512 devices in a mesh: rep: 16 (over z, core), fsdp: 32 (over y, x).
Axes of the slice: x: 4, y: 8, z: 8, core: 2. Of those that a mesh axis runs over, the one named last changes fastest.
Arguments:
- grad: bfloat16 [16, 4096, 3072], P('rep', 'fsdp'), may hold values from -50 to 50
- momentum: bfloat16 [16, 4096, 3072], P('rep', 'fsdp'), may hold values from -6 to 6
- kept_index: int32 [16, 64, 1536], P('rep', 'fsdp'), may hold values from 0 to 4095, as said below
- weights: bfloat16 [4096, 3072], P('fsdp'), may hold values from -3 to 3
Outputs:
- new_momentum: bfloat16 [16, 4096, 3072], P('rep', 'fsdp')
- new_weights: bfloat16 [4096, 3072], P('fsdp')
The draws below stay inside these ranges and needn't reach their ends.
Inputs may be any that keep to these rules, and one draw needn't show every extreme that they name: `kept_index`: the 32 positions of a group are distinct: the j-th lies among positions j * 128 to (j + 1) * 128 - 1.
All inputs are finite; a program needn't handle non-finite values.
Results may differ from the reference program's by a relative error of at most 0.001.
Values sent between devices are 32-bit elements; how exact they have to be, the bound alone decides.
No kernel may reach another device: no remote copies, remote signals or barrier semaphores. Data moves between devices by JAX's collectives and lax.ppermute only.
A program may use at most 64 MiB of HBM per device.

```python
import math
import jax
import jax.numpy as jnp
from jax import lax

K = 32
COLS = 3072
REPS = 16
ROWS = 4096


def draw_grad(key, part):
    key = jax.random.fold_in(key, 11)
    keys = jax.random.split(key, 3)
    shape = (REPS, ROWS, COLS)
    row_scale = jnp.exp(jax.random.uniform(keys[1], (REPS, ROWS, 1)) * math.log(10.0))
    col_scale = jnp.exp(jax.random.uniform(keys[2], (REPS, 1, COLS)) * math.log(10.0))
    rising = 1.0 + 0.732 * jnp.arange(ROWS, dtype=jnp.float32)[None, :, None] / max(ROWS - 1, 1)
    base = jnp.clip(jax.random.normal(keys[0], shape), -4.0, 4.0)
    return (base * rising * row_scale * col_scale / 28.8).astype(jnp.bfloat16)


def draw_kept_index(key, part):
    key = jax.random.fold_in(key, 23)
    shape = (REPS, ROWS // 64, COLS // 64 * K)
    stride = 4096 // K
    offset = jax.random.randint(key, shape, 0, stride)
    stratum = jnp.arange(shape[2], dtype=jnp.int32) % K
    return (offset + stratum * stride).astype(jnp.int32)


def shard_levels(stream_key, dims, cuts, low, top_value):
    factor_of, own = 1.0, jax.random.fold_in(stream_key, 6)
    for dim, blocks in cuts:
        draws = jnp.exp(jax.random.uniform(jax.random.fold_in(own, dim), (blocks,), jnp.float32, low / len(cuts), top_value / len(cuts)))
        factor_of = factor_of * jnp.repeat(draws, dims[dim] // blocks).reshape([-1 if axis == dim else 1 for axis in range(len(dims))])
    return factor_of


def centred(own_key, shape, scale, bound, cuts=(), kind=jnp.bfloat16):
    result = scale * jax.random.normal(own_key, shape, jnp.float32)
    if cuts:
        result = result * shard_levels(own_key, shape, cuts, -0.22, 0.18)
    return jnp.clip(result, -bound, bound).astype(kind)


def setup_inputs(seed: int = 0) -> dict:
    key_of = jax.random.split(jax.random.key(seed), 5)
    grad = draw_grad(jax.random.fold_in(key_of[4], 71), 0)
    momentum = centred(key_of[1], (REPS, ROWS, COLS), 1.0, 6.0, ((0, 16), (1, 32)))
    kept_index = draw_kept_index(jax.random.fold_in(key_of[4], 71), 0)
    weights = centred(key_of[3], (ROWS, COLS), 0.5, 3.0, ((0, 32),))
    return dict(grad=grad, momentum=momentum, kept_index=kept_index, weights=weights)


clip_rms = 0.5
momentum_decay = 0.9
step_rate = 0.5

def dct_table():
    frequency = jnp.arange(64, dtype=jnp.float32)[:, None]
    position = jnp.arange(64, dtype=jnp.float32)[None, :]
    weight = jnp.where(frequency == 0, jnp.sqrt(1.0 / 64.0), jnp.sqrt(2.0 / 64.0))
    return weight * jnp.cos(jnp.pi * (2.0 * position + 1.0) * frequency / 128.0)

def reference(grad, momentum, kept_index, weights):
    dct_rows = dct_table()
    high = lax.Precision.HIGHEST
    block_rows = ROWS // 64
    block_cols = COLS // 64

    def one_replica(running, inputs):
        grad_part, moment_part, index_part = inputs
        gradient = grad_part.astype(jnp.float32)
        mean_square = jnp.sum(gradient * gradient) / (ROWS * COLS)
        factor = jnp.minimum(1.0, clip_rms / jnp.sqrt(mean_square + 1e-06))
        blended = momentum_decay * moment_part.astype(jnp.float32) + factor * gradient
        grouped = blended.reshape(block_rows, 64, block_cols, 64)
        coeffs = jnp.einsum('ux,rxcy->rcuy', dct_rows, grouped, precision=high)
        coeffs = jnp.einsum('rcuy,vy->rcuv', coeffs, dct_rows, precision=high)
        coeffs = coeffs.reshape(block_rows, block_cols, 4096)
        kept_where = index_part.reshape(block_rows, block_cols, K)
        kept_values = jnp.take_along_axis(coeffs, kept_where, axis=2)
        row_pick = jnp.arange(block_rows)[:, None, None]
        col_pick = jnp.arange(block_cols)[None, :, None]
        sparse = jnp.zeros_like(coeffs).at[row_pick, col_pick, kept_where].set(kept_values)
        sparse = sparse.reshape(block_rows, block_cols, 64, 64)
        decoded = jnp.einsum('ux,rcuv->rcxv', dct_rows, sparse, precision=high)
        decoded = jnp.einsum('rcxv,vy->rxcy', decoded, dct_rows, precision=high).reshape(ROWS, COLS)
        return (running + decoded, (blended - decoded).astype(jnp.bfloat16))
    summed, new_momentum = lax.scan(one_replica, jnp.zeros((ROWS, COLS), jnp.float32), (grad, momentum, kept_index))
    new_weights = (weights.astype(jnp.float32) - step_rate * summed).astype(jnp.bfloat16)
    return (new_momentum, new_weights)
```

```python
import functools

import jax
import jax.numpy as jnp
import ml_dtypes
import numpy as np
from jax import lax
from jax.experimental import pallas as pl
from jax.experimental.pallas import tpu as pltpu
from jax.sharding import PartitionSpec as P

clip_rms = 0.5
momentum_decay = 0.9
step_rate = 0.5
VMEM = pltpu.VMEM
NN = (((1,), (0,)), ((), ()))
NT = (((1,), (1,)), ((), ()))


def split_table(table):
    high = table.astype(ml_dtypes.bfloat16)
    low = (table - high.astype(np.float64)).astype(ml_dtypes.bfloat16)
    return high, low


def tables():
    u = np.arange(64, dtype=np.float64)[:, None]
    x = np.arange(64, dtype=np.float64)[None, :]
    weight = np.where(u == 0, np.sqrt(1.0 / 64.0), np.sqrt(2.0 / 64.0))
    dct = weight * np.cos(np.pi * (2.0 * x + 1.0) * u / 128.0)
    pair = np.kron(np.eye(2), dct)
    rows = np.zeros((2, 64, 2, 2, 32))
    by_parity = dct.reshape(32, 2, 64)
    for i in range(2):
        rows[i, :, :, i, :] = by_parity.transpose(2, 1, 0)
    return pair, rows.reshape(128, 128)


def split(value):
    high = value.astype(jnp.bfloat16)
    low = (value - high.astype(jnp.float32)).astype(jnp.bfloat16)
    return high, low


def dot(left, right, dims):
    return lax.dot_general(left, right, dims, preferred_element_type=jnp.float32)


def duplicate(packed):
    lane = lax.broadcasted_iota(jnp.int32, packed.shape, 1)
    other = pltpu.roll(packed, 64, 1)
    return jnp.where(lane < 64, packed, other), jnp.where(lane < 64, other, packed)


def rows_of(offset):
    lane = lax.broadcasted_iota(jnp.int32, offset.shape, 1)
    return jnp.where((offset >> 6) == (lane >> 6), offset & 63, -1)


def square_kernel(grad_ref, out_ref):
    def step(k, total):
        at = pl.ds(pl.multiple_of(k * 256, 256), 256)
        value = grad_ref[:, at].astype(jnp.float32)
        value = value * value
        value = value[:, :128] + value[:, 128:]
        return total + jnp.sum(value.reshape(-1, 8, 128), axis=0)

    total = lax.fori_loop(
        0, grad_ref.shape[1] // 256, step, jnp.zeros((8, 128), jnp.float32), unroll=4
    )
    out_ref[...] = jnp.broadcast_to(
        jnp.sum(total, axis=0, keepdims=True)[None], out_ref.shape
    )


def pick_kernel(
    grad_ref, moment_ref, where_ref, forth_ref, pair_high_ref, pair_low_ref, out_ref, at_ref, kept_ref
):
    for h, offset in enumerate(duplicate(where_ref[...] & 127)):
        at_ref[h] = rows_of(offset)
    level = lax.broadcasted_iota(jnp.int32, (64, 128), 0)
    forth = forth_ref[...]
    pair_high, pair_low = pair_high_ref[...], pair_low_ref[...]

    def step(k, carry):
        at = pl.ds(pl.multiple_of(k * 128, 128), 128)
        both = jnp.concatenate([grad_ref[:, at], moment_ref[:, at]], axis=1)
        first = dot(forth, both, NN)
        first = first[:128] + first[128:]
        for n in range(2):
            high, low = split(first[:, n * 128 : (n + 1) * 128])
            coeffs = dot(pair_high, high, NT) + (dot(pair_high, low, NT) + dot(pair_low, high, NT))
            for h in range(2):
                hit = level == at_ref[h, pl.ds(k, 1), :]
                kept_ref[n, h, pl.ds(k, 1), :] = jnp.sum(
                    jnp.where(hit, coeffs[h * 64 : (h + 1) * 64], 0.0), axis=0, keepdims=True
                )
        return carry

    lax.fori_loop(0, grad_ref.shape[1] // 128, step, 0, unroll=2)
    lane = lax.broadcasted_iota(jnp.int32, out_ref.shape[1:], 1)
    for n in range(2):
        front, back = kept_ref[n, 0], kept_ref[n, 1]
        front = front + pltpu.roll(front, 64, 1)
        back = back + pltpu.roll(back, 64, 1)
        out_ref[n] = jnp.where(lane < 64, front, back)


def scale_kernel(count, squares_ref, picked_ref, where_ref, factor_ref, out_ref):
    total = jnp.sum(jnp.sum(squares_ref[...], axis=0), axis=1, keepdims=True)
    mean_square = jnp.broadcast_to(total, (1, 128)) / count
    factor = jnp.minimum(1.0, clip_rms / jnp.sqrt(mean_square + 1e-06))
    factor_ref[...] = factor
    groups = where_ref.shape[0]
    out_ref[:groups] = momentum_decay * picked_ref[1] + factor * picked_ref[0]
    out_ref[groups:] = (where_ref[...] & 127).astype(jnp.float32)


def decode(sparse, back_high_ref, back_low_ref, pair_high_ref, pair_low_ref):
    high, low = split(sparse)
    back_high, back_low = back_high_ref[...], back_low_ref[...]
    first = dot(back_high, high, NT) + (dot(back_high, low, NT) + dot(back_low, high, NT))
    high, low = split(first)
    pair_high, pair_low = pair_high_ref[...], pair_low_ref[...]
    return dot(high, pair_high, NN) + (dot(low, pair_high, NN) + dot(high, pair_low, NN))


def finish_kernel(
    own_ref,
    all_ref,
    factor_ref,
    grad_ref,
    moment_ref,
    weight_ref,
    back_high_ref,
    back_low_ref,
    pair_high_ref,
    pair_low_ref,
    new_moment_ref,
    new_weight_ref,
    at_ref,
    value_ref,
):
    replicas = all_ref.shape[0]
    groups = all_ref.shape[1] // 2
    table_refs = (back_high_ref, back_low_ref, pair_high_ref, pair_low_ref)
    for r in range(replicas + 1):
        listing = own_ref[...] if r == replicas else all_ref[r]
        values = duplicate(listing[:groups])
        offsets = duplicate(listing[groups:].astype(jnp.int32))
        for h in range(2):
            value_ref[r, h] = values[h]
            at_ref[r, h] = rows_of(offsets[h])
    level = lax.broadcasted_iota(jnp.int32, (64, 128), 0)
    factor = factor_ref[...]

    def term(r, h, k):
        hit = level == at_ref[r, h, pl.ds(k, 1), :]
        return jnp.where(hit, value_ref[r, h, pl.ds(k, 1), :], 0.0)

    def step(k, carry):
        at = pl.ds(pl.multiple_of(k * 128, 128), 128)
        own = jnp.concatenate([term(replicas, h, k) for h in range(2)], axis=0)
        blended = momentum_decay * moment_ref[:, at].astype(jnp.float32) + factor * grad_ref[
            :, at
        ].astype(jnp.float32)
        new_moment_ref[:, at] = (blended - decode(own, *table_refs)).astype(jnp.bfloat16)
        parts = []
        for h in range(2):
            total = term(0, h, k)
            for r in range(1, replicas):
                total = total + term(r, h, k)
            parts.append(total)
        update = decode(jnp.concatenate(parts, axis=0), *table_refs)
        new_weight_ref[:, at] = (
            weight_ref[:, at].astype(jnp.float32) - step_rate * update
        ).astype(jnp.bfloat16)
        return carry

    lax.fori_loop(0, groups, step, 0, unroll=2)


def body(grad, momentum, kept_index, weights):
    grad, momentum = grad[0], momentum[0]
    rows, cols = grad.shape
    ring = lax.axis_size("fsdp")
    replicas = lax.axis_size("rep")
    groups = cols // 128
    pair, back = tables()
    pair_high, pair_low = (jnp.asarray(t) for t in split_table(pair))
    back_high, back_low = (jnp.asarray(t) for t in split_table(back))
    forth = jnp.asarray(np.concatenate(split_table(back.T), axis=0))
    whole = pl.BlockSpec(memory_space=VMEM)
    params = pltpu.CompilerParams(vmem_limit_bytes=48 * 1024 * 1024)

    squares = pl.pallas_call(
        square_kernel,
        out_shape=jax.ShapeDtypeStruct((ring, 1, 128), jnp.float32),
        in_specs=[whole],
        out_specs=whole,
        compiler_params=params,
        name="squares",
    )(grad)
    squares = lax.all_to_all(squares, "fsdp", 0, 0, tiled=True)

    where = kept_index[0].reshape(2, groups, 2, 32).transpose(1, 2, 0, 3).reshape(groups, 128)
    picked = pl.pallas_call(
        pick_kernel,
        out_shape=jax.ShapeDtypeStruct((2, groups, 128), jnp.float32),
        in_specs=[whole] * 6,
        out_specs=whole,
        scratch_shapes=[
            VMEM((2, groups, 128), jnp.int32),
            VMEM((2, 2, groups, 128), jnp.float32),
        ],
        compiler_params=params,
        cost_estimate=pl.CostEstimate(
            flops=2 * 2 * 5 * 128 * 128 * cols, bytes_accessed=4 * rows * cols, transcendentals=0
        ),
        name="pick",
    )(grad, momentum, where, forth, pair_high, pair_low)

    factor, own = pl.pallas_call(
        functools.partial(scale_kernel, float(rows * ring * cols)),
        out_shape=(
            jax.ShapeDtypeStruct((1, 128), jnp.float32),
            jax.ShapeDtypeStruct((2 * groups, 128), jnp.float32),
        ),
        in_specs=[whole] * 3,
        out_specs=(whole, whole),
        compiler_params=params,
        name="scale",
    )(squares, picked, where)

    every = lax.all_gather(own, "rep", axis=0, tiled=False)

    new_momentum, new_weights = pl.pallas_call(
        finish_kernel,
        out_shape=(
            jax.ShapeDtypeStruct((rows, cols), jnp.bfloat16),
            jax.ShapeDtypeStruct((rows, cols), jnp.bfloat16),
        ),
        in_specs=[whole] * 10,
        out_specs=(whole, whole),
        scratch_shapes=[
            VMEM((replicas + 1, 2, groups, 128), jnp.int32),
            VMEM((replicas + 1, 2, groups, 128), jnp.float32),
        ],
        compiler_params=params,
        name="finish",
    )(own, every, factor, grad, momentum, weights, back_high, back_low, pair_high, pair_low)
    return (new_momentum[None], new_weights)


def solution(mesh):
    in_specs = (
        P("rep", "fsdp", None),
        P("rep", "fsdp", None),
        P("rep", "fsdp", None),
        P("fsdp", None),
    )
    out_specs = (P("rep", "fsdp", None), P("fsdp", None))
    return jax.shard_map(body, mesh=mesh, in_specs=in_specs, out_specs=out_specs, check_vma=False)
```

```python
import functools

import jax
import jax.numpy as jnp
import ml_dtypes
import numpy as np
from jax import lax
from jax.experimental import pallas as pl
from jax.experimental.pallas import tpu as pltpu
from jax.sharding import PartitionSpec as P

clip_rms = 0.5
momentum_decay = 0.9
step_rate = 0.5
VMEM = pltpu.VMEM
UNROLL = 24
NN = (((1,), (0,)), ((), ()))
NT = (((1,), (1,)), ((), ()))


def split_table(table):
    high = table.astype(ml_dtypes.bfloat16)
    low = (table - high.astype(np.float64)).astype(ml_dtypes.bfloat16)
    return high, low


def tables():
    u = np.arange(64, dtype=np.float64)[:, None]
    x = np.arange(64, dtype=np.float64)[None, :]
    weight = np.where(u == 0, np.sqrt(1.0 / 64.0), np.sqrt(2.0 / 64.0))
    dct = weight * np.cos(np.pi * (2.0 * x + 1.0) * u / 128.0)
    pair = np.kron(np.eye(2), dct)
    rows = np.zeros((2, 64, 2, 2, 32))
    by_parity = dct.reshape(32, 2, 64)
    for i in range(2):
        rows[i, :, :, i, :] = by_parity.transpose(2, 1, 0)
    return pair, rows.reshape(128, 128)


def widen(table):
    high, low = split_table(table)
    return np.block([[high, high], [low, low]])


def split(value):
    high = value.astype(jnp.bfloat16)
    low = (value - high.astype(jnp.float32)).astype(jnp.bfloat16)
    return high, low


def dot(left, right, dims):
    return lax.dot_general(left, right, dims, preferred_element_type=jnp.float32)


def duplicate(packed):
    lane = lax.broadcasted_iota(jnp.int32, packed.shape, 1)
    other = pltpu.roll(packed, 64, 1)
    return jnp.where(lane < 64, packed, other), jnp.where(lane < 64, other, packed)


def rows_of(offset):
    lane = lax.broadcasted_iota(jnp.int32, offset.shape, 1)
    return jnp.where((offset >> 6) == (lane >> 6), offset & 63, -1)


def stages(count, unroll, *steps):
    for step in steps:
        if unroll >= count:
            for k in range(count):
                step(k)
        else:
            lax.fori_loop(0, count, lambda k, carry, step=step: (step(k), carry)[1], 0, unroll=unroll)


def block(k):
    return pl.ds(k * 128 if isinstance(k, int) else pl.multiple_of(k * 128, 128), 128)


def row(k):
    return pl.ds(k, 1)


def square_kernel(grad_ref, out_ref):
    def step(k, total):
        value = grad_ref[:, block(k)].astype(jnp.float32)
        return total + jnp.sum((value * value).reshape(-1, 8, 128), axis=0)

    total = lax.fori_loop(
        0, grad_ref.shape[1] // 128, step, jnp.zeros((8, 128), jnp.float32), unroll=8
    )
    out_ref[...] = jnp.broadcast_to(
        jnp.sum(total, axis=0, keepdims=True)[None], out_ref.shape
    )


def pick_kernel(
    grad_ref, moment_ref, where_ref, forth_ref, pair_ref, out_ref, at_ref, first_ref, kept_ref
):
    groups = where_ref.shape[0]
    for h, offset in enumerate(duplicate(where_ref[...] & 127)):
        at_ref[h] = rows_of(offset)
    level = lax.broadcasted_iota(jnp.int32, (64, 128), 0)

    def over_rows(k):
        both = jnp.concatenate([grad_ref[:, block(k)], moment_ref[:, block(k)]], axis=1)
        first = dot(forth_ref[...], both, NN)
        high, low = split(first[:128] + first[128:])
        for n in range(2):
            first_ref[k, n * 128 : (n + 1) * 128, :128] = high[:, n * 128 : (n + 1) * 128]
            first_ref[k, n * 128 : (n + 1) * 128, 128:] = low[:, n * 128 : (n + 1) * 128]

    def over_columns(k):
        coeffs = dot(pair_ref[...], first_ref[k], NT)
        coeffs = coeffs[:128] + coeffs[128:]
        for h in range(2):
            hit = level == at_ref[h, row(k), :]
            for n in range(2):
                part = coeffs[h * 64 : (h + 1) * 64, n * 128 : (n + 1) * 128]
                kept_ref[n, h, row(k), :] = jnp.sum(
                    jnp.where(hit, part, 0.0), axis=0, keepdims=True
                )

    stages(groups, UNROLL, over_rows, over_columns)
    lane = lax.broadcasted_iota(jnp.int32, out_ref.shape[1:], 1)
    for n in range(2):
        front, back = kept_ref[n, 0], kept_ref[n, 1]
        front = front + pltpu.roll(front, 64, 1)
        back = back + pltpu.roll(back, 64, 1)
        out_ref[n] = jnp.where(lane < 64, front, back)


def scale_kernel(count, squares_ref, picked_ref, where_ref, factor_ref, out_ref):
    total = jnp.sum(jnp.sum(squares_ref[...], axis=0), axis=1, keepdims=True)
    mean_square = jnp.broadcast_to(total, (1, 128)) / count
    factor = jnp.minimum(1.0, clip_rms / jnp.sqrt(mean_square + 1e-06))
    factor_ref[...] = factor
    groups = where_ref.shape[0]
    out_ref[:groups] = momentum_decay * picked_ref[1] + factor * picked_ref[0]
    out_ref[groups:] = (where_ref[...] & 127).astype(jnp.float32)


def finish_kernel(
    own_ref,
    all_ref,
    factor_ref,
    grad_ref,
    moment_ref,
    weight_ref,
    back_ref,
    pair_ref,
    new_moment_ref,
    new_weight_ref,
    at_ref,
    value_ref,
    sparse_ref,
    first_ref,
):
    replicas = all_ref.shape[0]
    groups = all_ref.shape[1] // 2
    for r in range(replicas + 1):
        listing = own_ref[...] if r == replicas else all_ref[r]
        values = duplicate(listing[:groups])
        offsets = duplicate(listing[groups:].astype(jnp.int32))
        for h in range(2):
            value_ref[r, h] = values[h]
            at_ref[r, h] = rows_of(offsets[h])
    level = lax.broadcasted_iota(jnp.int32, (64, 128), 0)
    factor = factor_ref[...]

    def term(r, h, k):
        hit = level == at_ref[r, h, row(k), :]
        return jnp.where(hit, value_ref[r, h, row(k), :], 0.0)

    def scatter(k):
        for h in range(2):
            total = term(0, h, k)
            for r in range(1, replicas):
                total = total + term(r, h, k)
            for n, part in enumerate((term(replicas, h, k), total)):
                high, low = split(part)
                at = slice(n * 128 + h * 64, n * 128 + h * 64 + 64)
                sparse_ref[k, at, :128] = high
                sparse_ref[k, at, 128:] = low

    def over_rows(k):
        first = dot(back_ref[...], sparse_ref[k], NT)
        high, low = split(first[:128] + first[128:])
        for n in range(2):
            first_ref[k, n * 128 : (n + 1) * 128, :128] = high[:, n * 128 : (n + 1) * 128]
            first_ref[k, n * 128 : (n + 1) * 128, 128:] = low[:, n * 128 : (n + 1) * 128]

    def over_columns(k):
        decoded = dot(first_ref[k], pair_ref[...], NN)
        decoded = decoded[:, :128] + decoded[:, 128:]
        blended = momentum_decay * moment_ref[:, block(k)].astype(jnp.float32)
        blended = blended + factor * grad_ref[:, block(k)].astype(jnp.float32)
        new_moment_ref[:, block(k)] = (blended - decoded[:128]).astype(jnp.bfloat16)
        new_weight_ref[:, block(k)] = (
            weight_ref[:, block(k)].astype(jnp.float32) - step_rate * decoded[128:]
        ).astype(jnp.bfloat16)

    stages(groups, UNROLL, scatter, over_rows, over_columns)


def body(grad, momentum, kept_index, weights):
    grad, momentum = grad[0], momentum[0]
    rows, cols = grad.shape
    ring = lax.axis_size("fsdp")
    replicas = lax.axis_size("rep")
    groups = cols // 128
    pair, back = tables()
    forth = jnp.asarray(np.concatenate(split_table(back.T), axis=0))
    back_wide = jnp.asarray(widen(back))
    pair_wide = jnp.asarray(widen(pair))
    pair_tall = jnp.asarray(np.ascontiguousarray(widen(pair.T).T))
    whole = pl.BlockSpec(memory_space=VMEM)
    params = pltpu.CompilerParams(vmem_limit_bytes=48 * 1024 * 1024)

    squares = pl.pallas_call(
        square_kernel,
        out_shape=jax.ShapeDtypeStruct((ring, 1, 128), jnp.float32),
        in_specs=[whole],
        out_specs=whole,
        compiler_params=params,
        name="squares",
    )(grad)
    squares = lax.all_to_all(squares, "fsdp", 0, 0, tiled=True)

    where = kept_index[0].reshape(2, groups, 2, 32).transpose(1, 2, 0, 3).reshape(groups, 128)
    picked = pl.pallas_call(
        pick_kernel,
        out_shape=jax.ShapeDtypeStruct((2, groups, 128), jnp.float32),
        in_specs=[whole] * 5,
        out_specs=whole,
        scratch_shapes=[
            VMEM((2, groups, 128), jnp.int32),
            VMEM((groups, 256, 256), jnp.bfloat16),
            VMEM((2, 2, groups, 128), jnp.float32),
        ],
        compiler_params=params,
        cost_estimate=pl.CostEstimate(
            flops=2 * 2 * 5 * 128 * 128 * cols, bytes_accessed=4 * rows * cols, transcendentals=0
        ),
        name="pick",
    )(grad, momentum, where, forth, pair_wide)

    factor, own = pl.pallas_call(
        functools.partial(scale_kernel, float(rows * ring * cols)),
        out_shape=(
            jax.ShapeDtypeStruct((1, 128), jnp.float32),
            jax.ShapeDtypeStruct((2 * groups, 128), jnp.float32),
        ),
        in_specs=[whole] * 3,
        out_specs=(whole, whole),
        compiler_params=params,
        name="scale",
    )(squares, picked, where)

    every = lax.all_gather(own, "rep", axis=0, tiled=False)

    new_momentum, new_weights = pl.pallas_call(
        finish_kernel,
        out_shape=(
            jax.ShapeDtypeStruct((rows, cols), jnp.bfloat16),
            jax.ShapeDtypeStruct((rows, cols), jnp.bfloat16),
        ),
        in_specs=[whole] * 8,
        out_specs=(whole, whole),
        scratch_shapes=[
            VMEM((replicas + 1, 2, groups, 128), jnp.int32),
            VMEM((replicas + 1, 2, groups, 128), jnp.float32),
            VMEM((groups, 256, 256), jnp.bfloat16),
            VMEM((groups, 256, 256), jnp.bfloat16),
        ],
        compiler_params=params,
        name="finish",
    )(own, every, factor, grad, momentum, weights, back_wide, pair_tall)
    return (new_momentum[None], new_weights)


def solution(mesh):
    in_specs = (
        P("rep", "fsdp", None),
        P("rep", "fsdp", None),
        P("rep", "fsdp", None),
        P("fsdp", None),
    )
    out_specs = (P("rep", "fsdp", None), P("fsdp", None))
    return jax.shard_map(body, mesh=mesh, in_specs=in_specs, out_specs=out_specs, check_vma=False)
```

```python
import functools

import jax
import jax.numpy as jnp
import ml_dtypes
import numpy as np
from jax import lax
from jax.experimental import pallas as pl
from jax.experimental.pallas import tpu as pltpu
from jax.sharding import PartitionSpec as P

clip_rms = 0.5
momentum_decay = 0.9
step_rate = 0.5
VMEM = pltpu.VMEM
NN = (((1,), (0,)), ((), ()))
NT = (((1,), (1,)), ((), ()))


def split_table(table):
    high = table.astype(ml_dtypes.bfloat16)
    low = (table - high.astype(np.float64)).astype(ml_dtypes.bfloat16)
    return high, low


def tables():
    u = np.arange(64, dtype=np.float64)[:, None]
    x = np.arange(64, dtype=np.float64)[None, :]
    weight = np.where(u == 0, np.sqrt(1.0 / 64.0), np.sqrt(2.0 / 64.0))
    dct = weight * np.cos(np.pi * (2.0 * x + 1.0) * u / 128.0)
    pair = np.kron(np.eye(2), dct)
    rows = np.zeros((2, 64, 2, 2, 32))
    by_parity = dct.reshape(32, 2, 64)
    for i in range(2):
        rows[i, :, :, i, :] = by_parity.transpose(2, 1, 0)
    return pair, rows.reshape(128, 128)


def widen(table):
    high, low = split_table(table)
    return np.block([[high, high], [low, low]])


def split(value):
    high = value.astype(jnp.bfloat16)
    low = (value - high.astype(jnp.float32)).astype(jnp.bfloat16)
    return high, low


def dot(left, right, dims):
    return lax.dot_general(left, right, dims, preferred_element_type=jnp.float32)


def duplicate(packed):
    lane = lax.broadcasted_iota(jnp.int32, packed.shape, 1)
    other = pltpu.roll(packed, 64, 1)
    return jnp.where(lane < 64, packed, other), jnp.where(lane < 64, other, packed)


def block(k):
    return pl.ds(k * 128 if isinstance(k, int) else pl.multiple_of(k * 128, 128), 128)


def row(k):
    return pl.ds(k, 1)


def square_kernel(grad_ref, out_ref):
    def step(k, total):
        value = grad_ref[:, block(k)].astype(jnp.float32)
        return total + jnp.sum((value * value).reshape(-1, 8, 128), axis=0)

    total = lax.fori_loop(
        0, grad_ref.shape[1] // 128, step, jnp.zeros((8, 128), jnp.float32), unroll=8
    )
    out_ref[...] = jnp.broadcast_to(
        jnp.sum(total, axis=0, keepdims=True)[None], out_ref.shape
    )


def put_split(ref, index, value):
    high, low = split(value)
    for n in range(value.shape[1] // 128):
        ref[index, n * 128 : (n + 1) * 128, :128] = high[:, n * 128 : (n + 1) * 128]
        ref[index, n * 128 : (n + 1) * 128, 128:] = low[:, n * 128 : (n + 1) * 128]


def pick_kernel(
    grad_ref,
    moment_ref,
    where_ref,
    forth_ref,
    pair_ref,
    back_ref,
    pair_tall_ref,
    out_ref,
    rest_ref,
    at_ref,
    first_ref,
    sparse_ref,
    second_ref,
    kept_ref,
):
    groups = where_ref.shape[0]
    lane = lax.broadcasted_iota(jnp.int32, out_ref.shape[1:], 1)
    for h, offset in enumerate(duplicate((where_ref[...] & 127).astype(jnp.float32))):
        at_ref[h] = jnp.where(lane < 64, offset, offset - 64.0)
    level = lax.broadcasted_iota(jnp.int32, (64, 128), 0).astype(jnp.float32)

    def encode_rows(k):
        both = jnp.concatenate([grad_ref[:, block(k)], moment_ref[:, block(k)]], axis=1)
        first = dot(forth_ref[...], both, NN)
        put_split(first_ref, k, first[:128] + first[128:])

    def encode_columns(k):
        coeffs = dot(pair_ref[...], first_ref[k], NT)
        coeffs = coeffs[:128] + coeffs[128:]
        for h in range(2):
            hit = level == at_ref[h, row(k), :]
            for n in range(2):
                part = coeffs[h * 64 : (h + 1) * 64, n * 128 : (n + 1) * 128]
                part = jnp.where(hit, part, 0.0)
                kept_ref[n, h, row(k), :] = jnp.sum(part, axis=0, keepdims=True)
                high, low = split(part)
                at = slice(n * 128 + h * 64, n * 128 + h * 64 + 64)
                sparse_ref[k, at, :128] = high
                sparse_ref[k, at, 128:] = low

    def decode_rows(k):
        first = dot(back_ref[...], sparse_ref[k], NT)
        put_split(second_ref, k, first[:128] + first[128:])

    def decode_columns(k):
        decoded = dot(second_ref[k], pair_tall_ref[...], NN)
        decoded = decoded[:, :128] + decoded[:, 128:]
        rest_ref[0, :, block(k)] = grad_ref[:, block(k)].astype(jnp.float32) - decoded[:128]
        rest_ref[1, :, block(k)] = momentum_decay * (
            moment_ref[:, block(k)].astype(jnp.float32) - decoded[128:]
        )

    for step in (encode_rows, encode_columns, decode_rows, decode_columns):
        for k in range(groups):
            step(k)
    for n in range(2):
        front, back = kept_ref[n, 0], kept_ref[n, 1]
        front = front + pltpu.roll(front, 64, 1)
        back = back + pltpu.roll(back, 64, 1)
        out_ref[n] = jnp.where(lane < 64, front, back)


def scale_kernel(count, squares_ref, picked_ref, where_ref, factor_ref, out_ref):
    total = jnp.sum(jnp.sum(squares_ref[...], axis=0), axis=1, keepdims=True)
    mean_square = jnp.broadcast_to(total, (1, 128)) / count
    factor = jnp.minimum(1.0, clip_rms / jnp.sqrt(mean_square + 1e-06))
    factor_ref[...] = factor
    groups = where_ref.shape[0]
    out_ref[:groups] = momentum_decay * picked_ref[1] + factor * picked_ref[0]
    out_ref[groups:] = (where_ref[...] & 127).astype(jnp.float32)


def finish_kernel(
    all_ref,
    factor_ref,
    rest_ref,
    weight_ref,
    back_ref,
    pair_tall_ref,
    new_moment_ref,
    new_weight_ref,
    at_ref,
    value_ref,
    sparse_ref,
    second_ref,
    moment_out_ref,
    weight_out_ref,
    sems,
):
    replicas = all_ref.shape[0]
    groups = all_ref.shape[1] // 2
    factor = factor_ref[...]
    for k in range(groups):
        moment_out_ref[:, block(k)] = (
            rest_ref[1, :, block(k)] + factor * rest_ref[0, :, block(k)]
        ).astype(jnp.bfloat16)
    copies = [pltpu.make_async_copy(moment_out_ref, new_moment_ref, sems.at[0])]
    copies[0].start()

    lane = lax.broadcasted_iota(jnp.int32, (groups, 128), 1)
    offsets = [all_ref[r, groups:] for r in range(replicas)]
    for r in range(replicas):
        total = all_ref[r, :groups]
        for s in range(r):
            total = total + jnp.where(offsets[s] == offsets[r], all_ref[s, :groups], 0.0)
        values = duplicate(total)
        for h, offset in enumerate(duplicate(offsets[r])):
            value_ref[r, h] = values[h]
            at_ref[r, h] = jnp.where(lane < 64, offset, offset - 64.0)
    level = lax.broadcasted_iota(jnp.int32, (64, 128), 0).astype(jnp.float32)

    def scatter(t):
        for k in range(2):
            for h in range(2):
                part = jnp.zeros((64, 128), jnp.float32)
                for r in range(replicas):
                    hit = level == at_ref[r, h, row(2 * t + k), :]
                    part = jnp.where(hit, value_ref[r, h, row(2 * t + k), :], part)
                high, low = split(part)
                at = slice(k * 128 + h * 64, k * 128 + h * 64 + 64)
                sparse_ref[t, at, :128] = high
                sparse_ref[t, at, 128:] = low

    def decode_rows(t):
        first = dot(back_ref[...], sparse_ref[t], NT)
        put_split(second_ref, t, first[:128] + first[128:])

    def decode_columns(t):
        decoded = dot(second_ref[t], pair_tall_ref[...], NN)
        decoded = decoded[:, :128] + decoded[:, 128:]
        for k in range(2):
            at = block(2 * t + k)
            weight_out_ref[:, at] = (
                weight_ref[:, at].astype(jnp.float32) - step_rate * decoded[k * 128 : (k + 1) * 128]
            ).astype(jnp.bfloat16)

    pairs = groups // 2
    per_copy = max(1, pairs // 3)
    for t in range(pairs + 2):
        if t < pairs:
            scatter(t)
        if 1 <= t <= pairs:
            decode_rows(t - 1)
        if 2 <= t:
            decode_columns(t - 2)
            done = t - 1
            if done % per_copy == 0:
                at = pl.ds((done - per_copy) * 256, per_copy * 256)
                copies.append(
                    pltpu.make_async_copy(
                        weight_out_ref.at[:, at], new_weight_ref.at[:, at], sems.at[len(copies)]
                    )
                )
                copies[-1].start()
    for copy in copies:
        copy.wait()


def body(grad, momentum, kept_index, weights):
    grad, momentum = grad[0], momentum[0]
    rows, cols = grad.shape
    ring = lax.axis_size("fsdp")
    replicas = lax.axis_size("rep")
    groups = cols // 128
    pair, back = tables()
    forth = jnp.asarray(np.concatenate(split_table(back.T), axis=0))
    back_wide = jnp.asarray(widen(back))
    pair_wide = jnp.asarray(widen(pair))
    pair_tall = jnp.asarray(np.ascontiguousarray(widen(pair.T).T))
    whole = pl.BlockSpec(memory_space=VMEM)
    params = pltpu.CompilerParams(vmem_limit_bytes=32 * 1024 * 1024)

    squares = pl.pallas_call(
        square_kernel,
        out_shape=jax.ShapeDtypeStruct((ring, 1, 128), jnp.float32),
        in_specs=[whole],
        out_specs=whole,
        compiler_params=params,
        name="squares",
    )(grad)
    squares = lax.all_to_all(squares, "fsdp", 0, 0, tiled=True)

    where = kept_index[0].reshape(2, groups, 2, 32).transpose(1, 2, 0, 3).reshape(groups, 128)
    picked, rest = pl.pallas_call(
        pick_kernel,
        out_shape=(
            jax.ShapeDtypeStruct((2, groups, 128), jnp.float32),
            jax.ShapeDtypeStruct((2, rows, cols), jnp.float32),
        ),
        in_specs=[whole] * 7,
        out_specs=(whole, whole),
        scratch_shapes=[
            VMEM((2, groups, 128), jnp.float32),
            VMEM((groups, 256, 256), jnp.bfloat16),
            VMEM((groups, 256, 256), jnp.bfloat16),
            VMEM((groups, 256, 256), jnp.bfloat16),
            VMEM((2, 2, groups, 128), jnp.float32),
        ],
        compiler_params=params,
        cost_estimate=pl.CostEstimate(
            flops=2 * 2 * 20 * 128 * 128 * cols, bytes_accessed=4 * rows * cols, transcendentals=0
        ),
        name="pick",
    )(grad, momentum, where, forth, pair_wide, back_wide, pair_tall)

    factor, own = pl.pallas_call(
        functools.partial(scale_kernel, float(rows * ring * cols)),
        out_shape=(
            jax.ShapeDtypeStruct((1, 128), jnp.float32),
            jax.ShapeDtypeStruct((2 * groups, 128), jnp.float32),
        ),
        in_specs=[whole] * 3,
        out_specs=(whole, whole),
        compiler_params=params,
        name="scale",
    )(squares, picked, where)

    every = lax.all_gather(own, "rep", axis=0, tiled=False)

    hbm = pl.BlockSpec(memory_space=pl.ANY)
    new_momentum, new_weights = pl.pallas_call(
        finish_kernel,
        out_shape=(
            jax.ShapeDtypeStruct((rows, cols), jnp.bfloat16),
            jax.ShapeDtypeStruct((rows, cols), jnp.bfloat16),
        ),
        in_specs=[whole] * 6,
        out_specs=(hbm, hbm),
        scratch_shapes=[
            VMEM((replicas, 2, groups, 128), jnp.float32),
            VMEM((replicas, 2, groups, 128), jnp.float32),
            VMEM((groups // 2, 256, 256), jnp.bfloat16),
            VMEM((groups // 2, 256, 256), jnp.bfloat16),
            VMEM((rows, cols), jnp.bfloat16),
            VMEM((rows, cols), jnp.bfloat16),
            pltpu.SemaphoreType.DMA((groups // 2 + 1,)),
        ],
        compiler_params=params,
        name="finish",
    )(every, factor, rest, weights, back_wide, pair_tall)
    return (new_momentum[None], new_weights)


def solution(mesh):
    in_specs = (
        P("rep", "fsdp", None),
        P("rep", "fsdp", None),
        P("rep", "fsdp", None),
        P("fsdp", None),
    )
    out_specs = (P("rep", "fsdp", None), P("fsdp", None))
    return jax.shard_map(body, mesh=mesh, in_specs=in_specs, out_specs=out_specs, check_vma=False)
```

```python
import functools

import jax
import jax.numpy as jnp
import ml_dtypes
import numpy as np
from jax import lax
from jax.experimental import pallas as pl
from jax.experimental.pallas import tpu as pltpu
from jax.sharding import PartitionSpec as P

clip_rms = 0.5
momentum_decay = 0.9
step_rate = 0.5
VMEM = pltpu.VMEM
NN = (((1,), (0,)), ((), ()))
NT = (((1,), (1,)), ((), ()))


def split_table(table):
    high = table.astype(ml_dtypes.bfloat16)
    low = (table - high.astype(np.float64)).astype(ml_dtypes.bfloat16)
    return high, low


def tables():
    u = np.arange(64, dtype=np.float64)[:, None]
    x = np.arange(64, dtype=np.float64)[None, :]
    weight = np.where(u == 0, np.sqrt(1.0 / 64.0), np.sqrt(2.0 / 64.0))
    dct = weight * np.cos(np.pi * (2.0 * x + 1.0) * u / 128.0)
    pair = np.kron(np.eye(2), dct)
    rows = np.zeros((2, 64, 2, 2, 32))
    by_parity = dct.reshape(32, 2, 64)
    for i in range(2):
        rows[i, :, :, i, :] = by_parity.transpose(2, 1, 0)
    return pair, rows.reshape(128, 128)


def widen(table):
    high, low = split_table(table)
    return np.block([[high, high], [low, low]])


def split(value):
    high = value.astype(jnp.bfloat16)
    low = (value - high.astype(jnp.float32)).astype(jnp.bfloat16)
    return high, low


def dot(left, right, dims):
    return lax.dot_general(left, right, dims, preferred_element_type=jnp.float32)


def duplicate(packed):
    lane = lax.broadcasted_iota(jnp.int32, packed.shape, 1)
    other = pltpu.roll(packed, 64, 1)
    return jnp.where(lane < 64, packed, other), jnp.where(lane < 64, other, packed)


def block(k):
    return pl.ds(k * 128 if isinstance(k, int) else pl.multiple_of(k * 128, 128), 128)


def row(k):
    return pl.ds(k, 1)


def square_kernel(grad_ref, out_ref):
    def step(k, total):
        value = grad_ref[:, block(k)].astype(jnp.float32)
        return total + jnp.sum((value * value).reshape(-1, 8, 128), axis=0)

    total = lax.fori_loop(
        0, grad_ref.shape[1] // 128, step, jnp.zeros((8, 128), jnp.float32), unroll=8
    )
    out_ref[...] = jnp.broadcast_to(
        jnp.sum(total, axis=0, keepdims=True)[None], out_ref.shape
    )


def put_split(ref, index, value):
    high, low = split(value)
    for n in range(value.shape[1] // 128):
        ref[index, n * 128 : (n + 1) * 128, :128] = high[:, n * 128 : (n + 1) * 128]
        ref[index, n * 128 : (n + 1) * 128, 128:] = low[:, n * 128 : (n + 1) * 128]


def pick_kernel(
    where_ref,
    grad_hbm,
    moment_hbm,
    forth_hbm,
    pair_hbm,
    back_hbm,
    pair_tall_hbm,
    weight_hbm,
    out_ref,
    rest_ref,
    weight_ref,
    back_ref,
    pair_tall_ref,
    grad_ref,
    moment_ref,
    forth_ref,
    pair_ref,
    sems,
    at_ref,
    first_ref,
    sparse_ref,
    second_ref,
    kept_ref,
):
    copies = [
        pltpu.make_async_copy(source, target, sems.at[n])
        for n, (source, target) in enumerate(
            (
                (forth_hbm, forth_ref),
                (grad_hbm, grad_ref),
                (moment_hbm, moment_ref),
                (pair_hbm, pair_ref),
                (back_hbm, back_ref),
                (pair_tall_hbm, pair_tall_ref),
                (weight_hbm, weight_ref),
            )
        )
    ]
    for copy in copies:
        copy.start()
    groups = where_ref.shape[0]
    lane = lax.broadcasted_iota(jnp.int32, out_ref.shape[1:], 1)
    for h, offset in enumerate(duplicate((where_ref[...] & 127).astype(jnp.float32))):
        at_ref[h] = jnp.where(lane < 64, offset, offset - 64.0)
    level = lax.broadcasted_iota(jnp.int32, (64, 128), 0).astype(jnp.float32)

    def encode_rows(k):
        both = jnp.concatenate([grad_ref[:, block(k)], moment_ref[:, block(k)]], axis=1)
        first = dot(forth_ref[...], both, NN)
        put_split(first_ref, k, first[:128] + first[128:])

    def encode_columns(k):
        coeffs = dot(pair_ref[...], first_ref[k], NT)
        coeffs = coeffs[:128] + coeffs[128:]
        for h in range(2):
            hit = level == at_ref[h, row(k), :]
            for n in range(2):
                part = coeffs[h * 64 : (h + 1) * 64, n * 128 : (n + 1) * 128]
                part = jnp.where(hit, part, 0.0)
                kept_ref[n, h, row(k), :] = jnp.sum(part, axis=0, keepdims=True)
                high, low = split(part)
                at = slice(n * 128 + h * 64, n * 128 + h * 64 + 64)
                sparse_ref[k, at, :128] = high
                sparse_ref[k, at, 128:] = low

    def decode_rows(k):
        first = dot(back_ref[...], sparse_ref[k], NT)
        put_split(second_ref, k, first[:128] + first[128:])

    def decode_columns(k):
        decoded = dot(second_ref[k], pair_tall_ref[...], NN)
        decoded = decoded[:, :128] + decoded[:, 128:]
        rest_ref[0, :, block(k)] = grad_ref[:, block(k)].astype(jnp.float32) - decoded[:128]
        rest_ref[1, :, block(k)] = momentum_decay * (
            moment_ref[:, block(k)].astype(jnp.float32) - decoded[128:]
        )

    for needed, step in (
        (copies[:3], encode_rows),
        (copies[3:4], encode_columns),
        (copies[4:5], decode_rows),
        (copies[5:], decode_columns),
    ):
        for copy in needed:
            copy.wait()
        for k in range(groups):
            step(k)
    for n in range(2):
        front, back = kept_ref[n, 0], kept_ref[n, 1]
        front = front + pltpu.roll(front, 64, 1)
        back = back + pltpu.roll(back, 64, 1)
        out_ref[n] = jnp.where(lane < 64, front, back)


def scale_kernel(count, squares_ref, picked_ref, where_ref, factor_ref, out_ref):
    total = jnp.sum(jnp.sum(squares_ref[...], axis=0), axis=1, keepdims=True)
    mean_square = jnp.broadcast_to(total, (1, 128)) / count
    factor = jnp.minimum(1.0, clip_rms / jnp.sqrt(mean_square + 1e-06))
    factor_ref[...] = factor
    groups = where_ref.shape[0]
    out_ref[:groups] = momentum_decay * picked_ref[1] + factor * picked_ref[0]
    out_ref[groups:] = (where_ref[...] & 127).astype(jnp.float32)


def finish_kernel(
    all_ref,
    factor_ref,
    rest_ref,
    weight_ref,
    back_ref,
    pair_tall_ref,
    new_moment_ref,
    new_weight_ref,
    at_ref,
    value_ref,
    sparse_ref,
    second_ref,
    moment_out_ref,
    weight_out_ref,
    sems,
):
    replicas = all_ref.shape[0]
    groups = all_ref.shape[1] // 2
    factor = factor_ref[...]
    for k in range(groups):
        moment_out_ref[:, block(k)] = (
            rest_ref[1, :, block(k)] + factor * rest_ref[0, :, block(k)]
        ).astype(jnp.bfloat16)
    copies = [pltpu.make_async_copy(moment_out_ref, new_moment_ref, sems.at[0])]
    copies[0].start()

    lane = lax.broadcasted_iota(jnp.int32, (groups, 128), 1)
    offsets = [all_ref[r, groups:] for r in range(replicas)]
    for r in range(replicas):
        total = all_ref[r, :groups]
        for s in range(r):
            total = total + jnp.where(offsets[s] == offsets[r], all_ref[s, :groups], 0.0)
        values = duplicate(total)
        for h, offset in enumerate(duplicate(offsets[r])):
            value_ref[r, h] = values[h]
            at_ref[r, h] = jnp.where(lane < 64, offset, offset - 64.0)
    level = lax.broadcasted_iota(jnp.int32, (64, 128), 0).astype(jnp.float32)

    def scatter(t):
        for k in range(2):
            for h in range(2):
                part = jnp.zeros((64, 128), jnp.float32)
                for r in range(replicas):
                    hit = level == at_ref[r, h, row(2 * t + k), :]
                    part = jnp.where(hit, value_ref[r, h, row(2 * t + k), :], part)
                high, low = split(part)
                at = slice(k * 128 + h * 64, k * 128 + h * 64 + 64)
                sparse_ref[t, at, :128] = high
                sparse_ref[t, at, 128:] = low

    def decode_rows(t):
        first = dot(back_ref[...], sparse_ref[t], NT)
        put_split(second_ref, t, first[:128] + first[128:])

    def decode_columns(t):
        decoded = dot(second_ref[t], pair_tall_ref[...], NN)
        decoded = decoded[:, :128] + decoded[:, 128:]
        for k in range(2):
            at = block(2 * t + k)
            weight_out_ref[:, at] = (
                weight_ref[:, at].astype(jnp.float32) - step_rate * decoded[k * 128 : (k + 1) * 128]
            ).astype(jnp.bfloat16)

    pairs = groups // 2
    per_copy = max(1, pairs // 3)
    for t in range(pairs + 2):
        if t < pairs:
            scatter(t)
        if 1 <= t <= pairs:
            decode_rows(t - 1)
        if 2 <= t:
            decode_columns(t - 2)
            done = t - 1
            if done % per_copy == 0:
                at = pl.ds((done - per_copy) * 256, per_copy * 256)
                copies.append(
                    pltpu.make_async_copy(
                        weight_out_ref.at[:, at], new_weight_ref.at[:, at], sems.at[len(copies)]
                    )
                )
                copies[-1].start()
    for copy in copies:
        copy.wait()


def body(grad, momentum, kept_index, weights):
    grad, momentum = grad[0], momentum[0]
    rows, cols = grad.shape
    ring = lax.axis_size("fsdp")
    replicas = lax.axis_size("rep")
    groups = cols // 128
    pair, back = tables()
    forth = jnp.asarray(np.concatenate(split_table(back.T), axis=0))
    back_wide = jnp.asarray(widen(back))
    pair_wide = jnp.asarray(widen(pair))
    pair_tall = jnp.asarray(np.ascontiguousarray(widen(pair.T).T))
    whole = pl.BlockSpec(memory_space=VMEM)
    params = pltpu.CompilerParams(vmem_limit_bytes=32 * 1024 * 1024)

    squares = pl.pallas_call(
        square_kernel,
        out_shape=jax.ShapeDtypeStruct((ring, 1, 128), jnp.float32),
        in_specs=[whole],
        out_specs=whole,
        compiler_params=params,
        name="squares",
    )(grad)
    squares = lax.all_to_all(squares, "fsdp", 0, 0, tiled=True)

    where = kept_index[0].reshape(2, groups, 2, 32).transpose(1, 2, 0, 3).reshape(groups, 128)
    hbm = pl.BlockSpec(memory_space=pltpu.HBM)
    picked, rest, weights_near, back_near, tall_near = pl.pallas_call(
        pick_kernel,
        out_shape=(
            jax.ShapeDtypeStruct((2, groups, 128), jnp.float32),
            jax.ShapeDtypeStruct((2, rows, cols), jnp.float32),
            jax.ShapeDtypeStruct((rows, cols), jnp.bfloat16),
            jax.ShapeDtypeStruct((256, 256), jnp.bfloat16),
            jax.ShapeDtypeStruct((256, 256), jnp.bfloat16),
        ),
        in_specs=[whole] + [hbm] * 7,
        out_specs=(whole,) * 5,
        scratch_shapes=[
            VMEM((rows, cols), jnp.bfloat16),
            VMEM((rows, cols), jnp.bfloat16),
            VMEM((256, 128), jnp.bfloat16),
            VMEM((256, 256), jnp.bfloat16),
            pltpu.SemaphoreType.DMA((7,)),
            VMEM((2, groups, 128), jnp.float32),
            VMEM((groups, 256, 256), jnp.bfloat16),
            VMEM((groups, 256, 256), jnp.bfloat16),
            VMEM((groups, 256, 256), jnp.bfloat16),
            VMEM((2, 2, groups, 128), jnp.float32),
        ],
        compiler_params=params,
        cost_estimate=pl.CostEstimate(
            flops=2 * 2 * 20 * 128 * 128 * cols, bytes_accessed=4 * rows * cols, transcendentals=0
        ),
        name="pick",
    )(where, *(pltpu.with_memory_space_constraint(t, pltpu.HBM) for t in (grad, momentum, forth, pair_wide, back_wide, pair_tall, weights)))

    factor, own = pl.pallas_call(
        functools.partial(scale_kernel, float(rows * ring * cols)),
        out_shape=(
            jax.ShapeDtypeStruct((1, 128), jnp.float32),
            jax.ShapeDtypeStruct((2 * groups, 128), jnp.float32),
        ),
        in_specs=[whole] * 3,
        out_specs=(whole, whole),
        compiler_params=params,
        name="scale",
    )(squares, picked, where)

    every = lax.all_gather(own, "rep", axis=0, tiled=False)

    new_momentum, new_weights = pl.pallas_call(
        finish_kernel,
        out_shape=(
            jax.ShapeDtypeStruct((rows, cols), jnp.bfloat16),
            jax.ShapeDtypeStruct((rows, cols), jnp.bfloat16),
        ),
        in_specs=[whole] * 6,
        out_specs=(hbm, hbm),
        scratch_shapes=[
            VMEM((replicas, 2, groups, 128), jnp.float32),
            VMEM((replicas, 2, groups, 128), jnp.float32),
            VMEM((groups // 2, 256, 256), jnp.bfloat16),
            VMEM((groups // 2, 256, 256), jnp.bfloat16),
            VMEM((rows, cols), jnp.bfloat16),
            VMEM((rows, cols), jnp.bfloat16),
            pltpu.SemaphoreType.DMA((groups // 2 + 1,)),
        ],
        compiler_params=params,
        name="finish",
    )(every, factor, rest, weights_near, back_near, tall_near)
    return (new_momentum[None], new_weights)


def solution(mesh):
    in_specs = (
        P("rep", "fsdp", None),
        P("rep", "fsdp", None),
        P("rep", "fsdp", None),
        P("fsdp", None),
    )
    out_specs = (P("rep", "fsdp", None), P("fsdp", None))
    return jax.shard_map(body, mesh=mesh, in_specs=in_specs, out_specs=out_specs, check_vma=False)
```

```python
import functools

import jax
import jax.numpy as jnp
import ml_dtypes
import numpy as np
from jax import lax
from jax.experimental import pallas as pl
from jax.experimental.pallas import tpu as pltpu
from jax.sharding import PartitionSpec as P

clip_rms = 0.5
momentum_decay = 0.9
step_rate = 0.5
VMEM = pltpu.VMEM
PARTS = 6
NN = (((1,), (0,)), ((), ()))
NT = (((1,), (1,)), ((), ()))


def split_table(table):
    high = table.astype(ml_dtypes.bfloat16)
    low = (table - high.astype(np.float64)).astype(ml_dtypes.bfloat16)
    return high, low


def tables():
    u = np.arange(64, dtype=np.float64)[:, None]
    x = np.arange(64, dtype=np.float64)[None, :]
    weight = np.where(u == 0, np.sqrt(1.0 / 64.0), np.sqrt(2.0 / 64.0))
    dct = weight * np.cos(np.pi * (2.0 * x + 1.0) * u / 128.0)
    pair = np.kron(np.eye(2), dct)
    rows = np.zeros((2, 64, 2, 2, 32))
    by_parity = dct.reshape(32, 2, 64)
    for i in range(2):
        rows[i, :, :, i, :] = by_parity.transpose(2, 1, 0)
    return pair, rows.reshape(128, 128)


def widen(table):
    high, low = split_table(table)
    return np.block([[high, high], [low, low]])


def split(value):
    high = value.astype(jnp.bfloat16)
    low = (value - high.astype(jnp.float32)).astype(jnp.bfloat16)
    return high, low


def dot(left, right, dims):
    return lax.dot_general(left, right, dims, preferred_element_type=jnp.float32)


def duplicate(packed):
    lane = lax.broadcasted_iota(jnp.int32, packed.shape, 1)
    other = pltpu.roll(packed, 64, 1)
    return jnp.where(lane < 64, packed, other), jnp.where(lane < 64, other, packed)


def block(k):
    return pl.ds(k * 128 if isinstance(k, int) else pl.multiple_of(k * 128, 128), 128)


def row(k):
    return pl.ds(k, 1)


def in_hbm(*arrays):
    return [pltpu.with_memory_space_constraint(array, pltpu.HBM) for array in arrays]


def put_split(ref, value):
    high, low = split(value)
    for n in range(value.shape[1] // 128):
        ref[n * 128 : (n + 1) * 128, :128] = high[:, n * 128 : (n + 1) * 128]
        ref[n * 128 : (n + 1) * 128, 128:] = low[:, n * 128 : (n + 1) * 128]


def fetch_kernel(grad_hbm, *refs):
    count = (len(refs) - 3) // 2
    sources, (out_ref, grad_ref), (targets, sems) = refs[:count], refs[count : count + 2], (refs[count + 2 : -1], refs[-1])
    copies = [
        pltpu.make_async_copy(source, target, sems.at[n])
        for n, (source, target) in enumerate(zip((grad_hbm, *sources), (grad_ref, *targets)))
    ]
    for copy in copies:
        copy.start()
    copies[0].wait()

    def step(k, total):
        value = grad_ref[:, block(k)].astype(jnp.float32)
        return total + jnp.sum((value * value).reshape(-1, 8, 128), axis=0)

    total = lax.fori_loop(
        0, grad_ref.shape[1] // 128, step, jnp.zeros((8, 128), jnp.float32), unroll=8
    )
    out_ref[...] = jnp.broadcast_to(
        jnp.sum(total, axis=0, keepdims=True)[None], out_ref.shape
    )
    for copy in copies[1:]:
        copy.wait()


def pick_kernel(
    where_ref, grad_ref, moment_ref, forth_ref, pair_ref, out_ref, at_ref, first_ref, kept_ref
):
    groups = where_ref.shape[0]
    lane = lax.broadcasted_iota(jnp.int32, out_ref.shape[1:], 1)
    for h, offset in enumerate(duplicate((where_ref[...] & 127).astype(jnp.float32))):
        at_ref[h] = jnp.where(lane < 64, offset, offset - 64.0)
    level = lax.broadcasted_iota(jnp.int32, (64, 128), 0).astype(jnp.float32)

    def over_rows(k):
        both = jnp.concatenate([grad_ref[:, block(k)], moment_ref[:, block(k)]], axis=1)
        first = dot(forth_ref[...], both, NN)
        put_split(first_ref.at[k], first[:128] + first[128:])

    def over_columns(k):
        coeffs = dot(pair_ref[...], first_ref[k], NT)
        coeffs = coeffs[:128] + coeffs[128:]
        for h in range(2):
            hit = level == at_ref[h, row(k), :]
            for n in range(2):
                part = coeffs[h * 64 : (h + 1) * 64, n * 128 : (n + 1) * 128]
                kept_ref[n, h, row(k), :] = jnp.sum(
                    jnp.where(hit, part, 0.0), axis=0, keepdims=True
                )

    for step in (over_rows, over_columns):
        for k in range(groups):
            step(k)
    for n in range(2):
        front, back = kept_ref[n, 0], kept_ref[n, 1]
        front = front + pltpu.roll(front, 64, 1)
        back = back + pltpu.roll(back, 64, 1)
        out_ref[n] = jnp.where(lane < 64, front, back)


def scale_kernel(count, squares_ref, picked_ref, where_ref, factor_ref, own_ref, send_ref):
    total = jnp.sum(jnp.sum(squares_ref[...], axis=0), axis=1, keepdims=True)
    mean_square = jnp.broadcast_to(total, (1, 128)) / count
    factor = jnp.minimum(1.0, clip_rms / jnp.sqrt(mean_square + 1e-06))
    factor_ref[...] = factor
    values = momentum_decay * picked_ref[1] + factor * picked_ref[0]
    listing = jnp.concatenate([values, (where_ref[...] & 127).astype(jnp.float32)], axis=0)
    own_ref[...] = listing
    send_ref[...] = jnp.broadcast_to(listing[None], send_ref.shape)


def unpack(listings, at_ref, value_ref):
    groups = at_ref.shape[2]
    lane = lax.broadcasted_iota(jnp.int32, (groups, 128), 1)
    offsets = [listing[groups:] for listing in listings]
    for r in range(len(listings)):
        total = listings[r][:groups]
        for s in range(r):
            total = total + jnp.where(offsets[s] == offsets[r], listings[s][:groups], 0.0)
        values = duplicate(total)
        for h, offset in enumerate(duplicate(offsets[r])):
            value_ref[r, h] = values[h]
            at_ref[r, h] = jnp.where(lane < 64, offset, offset - 64.0)


def decode(at_ref, value_ref, sparse_ref, second_ref, back_ref, tall_ref, ready, emit):
    lists, _, groups, _ = at_ref.shape
    level = lax.broadcasted_iota(jnp.int32, (64, 128), 0).astype(jnp.float32)

    def scatter(t, carry):
        for k in range(2):
            for h in range(2):
                part = jnp.zeros((64, 128), jnp.float32)
                for r in range(lists):
                    hit = level == at_ref[r, h, row(2 * t + k), :]
                    part = jnp.where(hit, value_ref[r, h, row(2 * t + k), :], part)
                high, low = split(part)
                at = slice(k * 128 + h * 64, k * 128 + h * 64 + 64)
                sparse_ref[t, at, :128] = high
                sparse_ref[t, at, 128:] = low
        return carry

    lax.fori_loop(0, groups // 2, scatter, 0)
    for copy in ready:
        copy.wait()
    for t in range(groups // 2):
        first = dot(back_ref[...], sparse_ref[t], NT)
        put_split(second_ref.at[t], first[:128] + first[128:])
    for t in range(groups // 2):
        decoded = dot(second_ref[t], tall_ref[...], NN)
        decoded = decoded[:, :128] + decoded[:, 128:]
        for k in range(2):
            emit(2 * t + k, decoded[k * 128 : (k + 1) * 128])


def fetch(sems, *pairs):
    copies = [pltpu.make_async_copy(source, target, sems.at[n]) for n, (source, target) in enumerate(pairs)]
    for copy in copies:
        copy.start()
    return copies


class Outlet:
    def __init__(self, source, target, sems, first_sem):
        self.source, self.target, self.sems, self.first_sem = source, target, sems, first_sem
        self.per = max(2, source.shape[1] // 128 // PARTS)
        self.copies = []

    def put(self, k, value):
        self.source[:, block(k)] = value.astype(self.source.dtype)
        if (k + 1) % self.per == 0:
            at = pl.ds((k + 1 - self.per) * 128, self.per * 128)
            copy = pltpu.make_async_copy(
                self.source.at[:, at],
                self.target.at[:, at],
                self.sems.at[self.first_sem + len(self.copies)],
            )
            copy.start()
            self.copies.append(copy)

    def wait(self):
        for copy in self.copies:
            copy.wait()


def own_kernel(
    own_ref, factor_ref, grad_ref, moment_ref, back_hbm, tall_hbm, new_moment_hbm,
    back_ref, tall_ref, at_ref, value_ref, sparse_ref, second_ref, out_ref, sems,
):
    ready = fetch(sems, (back_hbm, back_ref), (tall_hbm, tall_ref))
    factor = factor_ref[...]
    unpack([own_ref[...]], at_ref, value_ref)
    outlet = Outlet(out_ref, new_moment_hbm, sems, 2)

    def emit(k, decoded):
        blended = momentum_decay * moment_ref[:, block(k)].astype(jnp.float32)
        blended = blended + factor * grad_ref[:, block(k)].astype(jnp.float32)
        outlet.put(k, blended - decoded)

    decode(at_ref, value_ref, sparse_ref, second_ref, back_ref, tall_ref, ready, emit)
    outlet.wait()


def finish_kernel(
    all_ref, back_hbm, tall_hbm, weight_hbm, new_weight_hbm,
    back_ref, tall_ref, weight_ref, at_ref, value_ref, sparse_ref, second_ref, out_ref, sems,
):
    ready = fetch(sems, (back_hbm, back_ref), (tall_hbm, tall_ref), (weight_hbm, weight_ref))
    unpack([all_ref[r] for r in range(all_ref.shape[0])], at_ref, value_ref)
    outlet = Outlet(out_ref, new_weight_hbm, sems, 3)

    def emit(k, decoded):
        outlet.put(k, weight_ref[:, block(k)].astype(jnp.float32) - step_rate * decoded)

    decode(at_ref, value_ref, sparse_ref, second_ref, back_ref, tall_ref, ready, emit)
    outlet.wait()


def ring_order(size):
    head = size // 2 + 2 if size == 32 else 0
    return [head] + [member for member in range(size) if member != head]


def replica_order(size):
    return [chip * 2 + core for chip in range(size // 2 - 1, -1, -1) for core in range(2)]


def body(grad, momentum, kept_index, weights):
    grad, momentum = grad[0], momentum[0]
    rows, cols = grad.shape
    ring = lax.axis_size("fsdp")
    replicas = lax.axis_size("rep")
    groups = cols // 128
    bf16, f32 = jnp.bfloat16, jnp.float32
    pair, back = tables()
    forth = jnp.asarray(np.concatenate(split_table(back.T), axis=0))
    back_wide = jnp.asarray(widen(back))
    pair_wide = jnp.asarray(widen(pair))
    pair_tall = jnp.asarray(np.ascontiguousarray(widen(pair.T).T))
    whole = pl.BlockSpec(memory_space=VMEM)
    hbm = pl.BlockSpec(memory_space=pl.ANY)
    params = pltpu.CompilerParams(vmem_limit_bytes=32 * 1024 * 1024)
    full = jax.ShapeDtypeStruct((rows, cols), bf16)
    square = jax.ShapeDtypeStruct((256, 256), bf16)

    squares, grad_near, moment_near, kept_near, forth_near, pair_near = pl.pallas_call(
        fetch_kernel,
        out_shape=(
            jax.ShapeDtypeStruct((ring, 1, 128), f32),
            full,
            full,
            jax.ShapeDtypeStruct(kept_index.shape[1:], jnp.int32),
            jax.ShapeDtypeStruct((256, 128), bf16),
            square,
        ),
        in_specs=[hbm] * 5,
        out_specs=(whole,) * 6,
        scratch_shapes=[pltpu.SemaphoreType.DMA((5,))],
        compiler_params=params,
        name="fetch",
    )(*in_hbm(grad, momentum, kept_index[0], forth, pair_wide))
    squares = lax.all_to_all(
        squares, "fsdp", 0, 0, tiled=True, axis_index_groups=[ring_order(ring)]
    )

    where = kept_near.reshape(2, groups, 2, 32).transpose(1, 2, 0, 3).reshape(groups, 128)
    picked = pl.pallas_call(
        pick_kernel,
        out_shape=jax.ShapeDtypeStruct((2, groups, 128), f32),
        in_specs=[whole] * 5,
        out_specs=whole,
        scratch_shapes=[
            VMEM((2, groups, 128), f32),
            VMEM((groups, 256, 256), bf16),
            VMEM((2, 2, groups, 128), f32),
        ],
        compiler_params=params,
        cost_estimate=pl.CostEstimate(
            flops=2 * 2 * 10 * 128 * 128 * cols, bytes_accessed=4 * rows * cols, transcendentals=0
        ),
        name="pick",
    )(where, grad_near, moment_near, forth_near, pair_near)

    factor, own, send = pl.pallas_call(
        functools.partial(scale_kernel, float(rows * ring * cols)),
        out_shape=(
            jax.ShapeDtypeStruct((1, 128), f32),
            jax.ShapeDtypeStruct((2 * groups, 128), f32),
            jax.ShapeDtypeStruct((replicas, 2 * groups, 128), f32),
        ),
        in_specs=[whole] * 3,
        out_specs=(whole,) * 3,
        compiler_params=params,
        name="scale",
    )(squares, picked, where)

    every = lax.all_to_all(
        send, "rep", 0, 0, tiled=True, axis_index_groups=[replica_order(replicas)]
    )

    def work(lists):
        return [
            VMEM((lists, 2, groups, 128), f32),
            VMEM((lists, 2, groups, 128), f32),
            VMEM((groups // 2, 256, 256), bf16),
            VMEM((groups // 2, 256, 256), bf16),
            VMEM((rows, cols), bf16),
            pltpu.SemaphoreType.DMA((3 + groups // 2,)),
        ]

    new_momentum = pl.pallas_call(
        own_kernel,
        out_shape=full,
        in_specs=[whole] * 4 + [hbm] * 2,
        out_specs=hbm,
        scratch_shapes=[VMEM((256, 256), bf16)] * 2 + work(1),
        compiler_params=params,
        cost_estimate=pl.CostEstimate(
            flops=2 * 2 * 10 * 128 * 128 * cols, bytes_accessed=4 * rows * cols, transcendentals=0
        ),
        name="own",
    )(own, factor, grad_near, moment_near, *in_hbm(back_wide, pair_tall))

    new_weights = pl.pallas_call(
        finish_kernel,
        out_shape=full,
        in_specs=[whole] + [hbm] * 3,
        out_specs=hbm,
        scratch_shapes=[VMEM((256, 256), bf16)] * 2 + [VMEM((rows, cols), bf16)] + work(replicas),
        compiler_params=params,
        name="finish",
    )(every, *in_hbm(back_wide, pair_tall, weights))
    return (new_momentum[None], new_weights)


def solution(mesh):
    in_specs = (
        P("rep", "fsdp", None),
        P("rep", "fsdp", None),
        P("rep", "fsdp", None),
        P("fsdp", None),
    )
    out_specs = (P("rep", "fsdp", None), P("fsdp", None))
    return jax.shard_map(body, mesh=mesh, in_specs=in_specs, out_specs=out_specs, check_vma=False)
```

```python
import functools

import jax
import jax.numpy as jnp
import ml_dtypes
import numpy as np
from jax import lax
from jax.experimental import pallas as pl
from jax.experimental.pallas import tpu as pltpu
from jax.sharding import PartitionSpec as P

clip_rms = 0.5
momentum_decay = 0.9
step_rate = 0.5
VMEM = pltpu.VMEM
PARTS = 6
ZHEAD = 5
NN = (((1,), (0,)), ((), ()))
NT = (((1,), (1,)), ((), ()))


def split_table(table):
    high = table.astype(ml_dtypes.bfloat16)
    low = (table - high.astype(np.float64)).astype(ml_dtypes.bfloat16)
    return high, low


def tables():
    u = np.arange(64, dtype=np.float64)[:, None]
    x = np.arange(64, dtype=np.float64)[None, :]
    weight = np.where(u == 0, np.sqrt(1.0 / 64.0), np.sqrt(2.0 / 64.0))
    dct = weight * np.cos(np.pi * (2.0 * x + 1.0) * u / 128.0)
    pair = np.kron(np.eye(2), dct)
    rows = np.zeros((2, 64, 2, 2, 32))
    by_parity = dct.reshape(32, 2, 64)
    for i in range(2):
        rows[i, :, :, i, :] = by_parity.transpose(2, 1, 0)
    return pair, rows.reshape(128, 128)


def widen(table):
    high, low = split_table(table)
    return np.block([[high, high], [low, low]])


def split(value):
    high = value.astype(jnp.bfloat16)
    low = (value - high.astype(jnp.float32)).astype(jnp.bfloat16)
    return high, low


def dot(left, right, dims):
    return lax.dot_general(left, right, dims, preferred_element_type=jnp.float32)


def duplicate(packed):
    lane = lax.broadcasted_iota(jnp.int32, packed.shape, 1)
    other = pltpu.roll(packed, 64, 1)
    return jnp.where(lane < 64, packed, other), jnp.where(lane < 64, other, packed)


def block(k):
    return pl.ds(k * 128 if isinstance(k, int) else pl.multiple_of(k * 128, 128), 128)


def row(k):
    return pl.ds(k, 1)


def in_hbm(*arrays):
    return [pltpu.with_memory_space_constraint(array, pltpu.HBM) for array in arrays]


def put_split(ref, value):
    high, low = split(value)
    for n in range(value.shape[1] // 128):
        ref[n * 128 : (n + 1) * 128, :128] = high[:, n * 128 : (n + 1) * 128]
        ref[n * 128 : (n + 1) * 128, 128:] = low[:, n * 128 : (n + 1) * 128]


def fetch_kernel(grad_hbm, *refs):
    count = (len(refs) - 3) // 2
    sources, (out_ref, grad_ref), (targets, sems) = refs[:count], refs[count : count + 2], (refs[count + 2 : -1], refs[-1])
    copies = [
        pltpu.make_async_copy(source, target, sems.at[n])
        for n, (source, target) in enumerate(zip((grad_hbm, *sources), (grad_ref, *targets)))
    ]
    for copy in copies:
        copy.start()
    copies[0].wait()

    def step(k, total):
        value = grad_ref[:, block(k)].astype(jnp.float32)
        return total + jnp.sum((value * value).reshape(-1, 8, 128), axis=0)

    total = lax.fori_loop(
        0, grad_ref.shape[1] // 128, step, jnp.zeros((8, 128), jnp.float32), unroll=8
    )
    out_ref[...] = jnp.broadcast_to(
        jnp.sum(total, axis=0, keepdims=True)[None], out_ref.shape
    )
    for copy in copies[1:]:
        copy.wait()


def pick_kernel(
    where_ref, grad_ref, moment_ref, forth_ref, pair_ref, out_ref, at_ref, first_ref, kept_ref
):
    groups = where_ref.shape[0]
    lane = lax.broadcasted_iota(jnp.int32, out_ref.shape[1:], 1)
    for h, offset in enumerate(duplicate((where_ref[...] & 127).astype(jnp.float32))):
        at_ref[h] = jnp.where(lane < 64, offset, offset - 64.0)
    level = lax.broadcasted_iota(jnp.int32, (64, 128), 0).astype(jnp.float32)

    def over_rows(k):
        both = jnp.concatenate([grad_ref[:, block(k)], moment_ref[:, block(k)]], axis=1)
        first = dot(forth_ref[...], both, NN)
        put_split(first_ref.at[k], first[:128] + first[128:])

    def over_columns(k):
        coeffs = dot(pair_ref[...], first_ref[k], NT)
        coeffs = coeffs[:128] + coeffs[128:]
        for h in range(2):
            hit = level == at_ref[h, row(k), :]
            for n in range(2):
                part = coeffs[h * 64 : (h + 1) * 64, n * 128 : (n + 1) * 128]
                kept_ref[n, h, row(k), :] = jnp.sum(
                    jnp.where(hit, part, 0.0), axis=0, keepdims=True
                )

    for step in (over_rows, over_columns):
        for k in range(groups):
            step(k)
    for n in range(2):
        front, back = kept_ref[n, 0], kept_ref[n, 1]
        front = front + pltpu.roll(front, 64, 1)
        back = back + pltpu.roll(back, 64, 1)
        out_ref[n] = jnp.where(lane < 64, front, back)


def scale_kernel(count, squares_ref, picked_ref, where_ref, factor_ref, own_ref, send_ref):
    total = jnp.sum(jnp.sum(squares_ref[...], axis=0), axis=1, keepdims=True)
    mean_square = jnp.broadcast_to(total, (1, 128)) / count
    factor = jnp.minimum(1.0, clip_rms / jnp.sqrt(mean_square + 1e-06))
    factor_ref[...] = factor
    values = momentum_decay * picked_ref[1] + factor * picked_ref[0]
    listing = jnp.concatenate([values, (where_ref[...] & 127).astype(jnp.float32)], axis=0)
    own_ref[...] = listing
    send_ref[...] = jnp.broadcast_to(listing[None], send_ref.shape)


def unpack(listings, at_ref, value_ref):
    groups = at_ref.shape[2]
    lane = lax.broadcasted_iota(jnp.int32, (groups, 128), 1)
    offsets = [listing[groups:] for listing in listings]
    for r in range(len(listings)):
        total = listings[r][:groups]
        for s in range(r):
            total = total + jnp.where(offsets[s] == offsets[r], listings[s][:groups], 0.0)
        values = duplicate(total)
        for h, offset in enumerate(duplicate(offsets[r])):
            value_ref[r, h] = values[h]
            at_ref[r, h] = jnp.where(lane < 64, offset, offset - 64.0)


def decode(at_ref, value_ref, sparse_ref, second_ref, back_ref, tall_ref, ready, emit):
    lists, _, groups, _ = at_ref.shape
    level = lax.broadcasted_iota(jnp.int32, (64, 128), 0).astype(jnp.float32)

    def scatter(t, carry):
        for k in range(2):
            for h in range(2):
                part = jnp.zeros((64, 128), jnp.float32)
                for r in range(lists):
                    hit = level == at_ref[r, h, row(2 * t + k), :]
                    part = jnp.where(hit, value_ref[r, h, row(2 * t + k), :], part)
                high, low = split(part)
                at = slice(k * 128 + h * 64, k * 128 + h * 64 + 64)
                sparse_ref[t, at, :128] = high
                sparse_ref[t, at, 128:] = low
        return carry

    lax.fori_loop(0, groups // 2, scatter, 0)
    for copy in ready:
        copy.wait()
    for t in range(groups // 2):
        first = dot(back_ref[...], sparse_ref[t], NT)
        put_split(second_ref.at[t], first[:128] + first[128:])
    for t in range(groups // 2):
        decoded = dot(second_ref[t], tall_ref[...], NN)
        decoded = decoded[:, :128] + decoded[:, 128:]
        for k in range(2):
            emit(2 * t + k, decoded[k * 128 : (k + 1) * 128])


def fetch(sems, *pairs):
    copies = [pltpu.make_async_copy(source, target, sems.at[n]) for n, (source, target) in enumerate(pairs)]
    for copy in copies:
        copy.start()
    return copies


class Outlet:
    def __init__(self, source, target, sems, first_sem):
        self.source, self.target, self.sems, self.first_sem = source, target, sems, first_sem
        self.per = max(2, source.shape[1] // 128 // PARTS)
        self.copies = []

    def put(self, k, value):
        self.source[:, block(k)] = value.astype(self.source.dtype)
        if (k + 1) % self.per == 0:
            at = pl.ds((k + 1 - self.per) * 128, self.per * 128)
            copy = pltpu.make_async_copy(
                self.source.at[:, at],
                self.target.at[:, at],
                self.sems.at[self.first_sem + len(self.copies)],
            )
            copy.start()
            self.copies.append(copy)

    def wait(self):
        for copy in self.copies:
            copy.wait()


def own_kernel(
    own_ref, factor_ref, grad_ref, moment_ref, back_hbm, tall_hbm, new_moment_hbm,
    back_ref, tall_ref, at_ref, value_ref, sparse_ref, second_ref, out_ref, sems,
):
    ready = fetch(sems, (back_hbm, back_ref), (tall_hbm, tall_ref))
    factor = factor_ref[...]
    unpack([own_ref[...]], at_ref, value_ref)
    outlet = Outlet(out_ref, new_moment_hbm, sems, 2)

    def emit(k, decoded):
        blended = momentum_decay * moment_ref[:, block(k)].astype(jnp.float32)
        blended = blended + factor * grad_ref[:, block(k)].astype(jnp.float32)
        outlet.put(k, blended - decoded)

    decode(at_ref, value_ref, sparse_ref, second_ref, back_ref, tall_ref, ready, emit)
    outlet.wait()


def finish_kernel(
    all_ref, back_hbm, tall_hbm, weight_hbm, new_weight_hbm,
    back_ref, tall_ref, weight_ref, at_ref, value_ref, sparse_ref, second_ref, out_ref, sems,
):
    ready = fetch(sems, (back_hbm, back_ref), (tall_hbm, tall_ref), (weight_hbm, weight_ref))
    unpack([all_ref[r] for r in range(all_ref.shape[0])], at_ref, value_ref)
    outlet = Outlet(out_ref, new_weight_hbm, sems, 3)

    def emit(k, decoded):
        outlet.put(k, weight_ref[:, block(k)].astype(jnp.float32) - step_rate * decoded)

    decode(at_ref, value_ref, sparse_ref, second_ref, back_ref, tall_ref, ready, emit)
    outlet.wait()


def ring_order(size):
    head = size // 2 + 2 if size == 32 else 0
    return [head] + [member for member in range(size) if member != head]


def chip_order(size):
    head = ZHEAD % size
    return [(head - n) % size for n in range(size)]


def body(grad, momentum, kept_index, weights):
    grad, momentum = grad[0], momentum[0]
    rows, cols = grad.shape
    ring = lax.axis_size("fsdp")
    replicas = lax.axis_size("rep")
    groups = cols // 128
    bf16, f32 = jnp.bfloat16, jnp.float32
    pair, back = tables()
    forth = jnp.asarray(np.concatenate(split_table(back.T), axis=0))
    back_wide = jnp.asarray(widen(back))
    pair_wide = jnp.asarray(widen(pair))
    pair_tall = jnp.asarray(np.ascontiguousarray(widen(pair.T).T))
    whole = pl.BlockSpec(memory_space=VMEM)
    hbm = pl.BlockSpec(memory_space=pl.ANY)
    params = pltpu.CompilerParams(vmem_limit_bytes=32 * 1024 * 1024)
    full = jax.ShapeDtypeStruct((rows, cols), bf16)
    square = jax.ShapeDtypeStruct((256, 256), bf16)

    squares, grad_near, moment_near, kept_near, forth_near, pair_near = pl.pallas_call(
        fetch_kernel,
        out_shape=(
            jax.ShapeDtypeStruct((ring, 1, 128), f32),
            full,
            full,
            jax.ShapeDtypeStruct(kept_index.shape[1:], jnp.int32),
            jax.ShapeDtypeStruct((256, 128), bf16),
            square,
        ),
        in_specs=[hbm] * 5,
        out_specs=(whole,) * 6,
        scratch_shapes=[pltpu.SemaphoreType.DMA((5,))],
        compiler_params=params,
        name="fetch",
    )(*in_hbm(grad, momentum, kept_index[0], forth, pair_wide))
    squares = lax.all_to_all(
        squares, "fsdp", 0, 0, tiled=True, axis_index_groups=[ring_order(ring)]
    )

    where = kept_near.reshape(2, groups, 2, 32).transpose(1, 2, 0, 3).reshape(groups, 128)
    picked = pl.pallas_call(
        pick_kernel,
        out_shape=jax.ShapeDtypeStruct((2, groups, 128), f32),
        in_specs=[whole] * 5,
        out_specs=whole,
        scratch_shapes=[
            VMEM((2, groups, 128), f32),
            VMEM((groups, 256, 256), bf16),
            VMEM((2, 2, groups, 128), f32),
        ],
        compiler_params=params,
        cost_estimate=pl.CostEstimate(
            flops=2 * 2 * 10 * 128 * 128 * cols, bytes_accessed=4 * rows * cols, transcendentals=0
        ),
        name="pick",
    )(where, grad_near, moment_near, forth_near, pair_near)

    factor, own, send = pl.pallas_call(
        functools.partial(scale_kernel, float(rows * ring * cols)),
        out_shape=(
            jax.ShapeDtypeStruct((1, 128), f32),
            jax.ShapeDtypeStruct((2 * groups, 128), f32),
            jax.ShapeDtypeStruct((replicas // 2, 2 * groups, 128), f32),
        ),
        in_specs=[whole] * 3,
        out_specs=(whole,) * 3,
        compiler_params=params,
        name="scale",
    )(squares, picked, where)

    by_core = [[chip * 2 + core for chip in chip_order(replicas // 2)] for core in range(2)]
    every = lax.all_to_all(send, "rep", 0, 0, tiled=True, axis_index_groups=by_core)
    cores = [[chip * 2 + core for core in range(2)] for chip in range(replicas // 2)]
    every = lax.all_gather(every, "rep", axis=0, tiled=True, axis_index_groups=cores)

    def work(lists):
        return [
            VMEM((lists, 2, groups, 128), f32),
            VMEM((lists, 2, groups, 128), f32),
            VMEM((groups // 2, 256, 256), bf16),
            VMEM((groups // 2, 256, 256), bf16),
            VMEM((rows, cols), bf16),
            pltpu.SemaphoreType.DMA((3 + groups // 2,)),
        ]

    new_momentum = pl.pallas_call(
        own_kernel,
        out_shape=full,
        in_specs=[whole] * 4 + [hbm] * 2,
        out_specs=hbm,
        scratch_shapes=[VMEM((256, 256), bf16)] * 2 + work(1),
        compiler_params=params,
        cost_estimate=pl.CostEstimate(
            flops=2 * 2 * 10 * 128 * 128 * cols, bytes_accessed=4 * rows * cols, transcendentals=0
        ),
        name="own",
    )(own, factor, grad_near, moment_near, *in_hbm(back_wide, pair_tall))

    new_weights = pl.pallas_call(
        finish_kernel,
        out_shape=full,
        in_specs=[whole] + [hbm] * 3,
        out_specs=hbm,
        scratch_shapes=[VMEM((256, 256), bf16)] * 2 + [VMEM((rows, cols), bf16)] + work(replicas),
        compiler_params=params,
        name="finish",
    )(every, *in_hbm(back_wide, pair_tall, weights))
    return (new_momentum[None], new_weights)


def solution(mesh):
    in_specs = (
        P("rep", "fsdp", None),
        P("rep", "fsdp", None),
        P("rep", "fsdp", None),
        P("fsdp", None),
    )
    out_specs = (P("rep", "fsdp", None), P("fsdp", None))
    return jax.shard_map(body, mesh=mesh, in_specs=in_specs, out_specs=out_specs, check_vma=False)
```

```python
import functools

import jax
import jax.numpy as jnp
import ml_dtypes
import numpy as np
from jax import lax
from jax.experimental import pallas as pl
from jax.experimental.pallas import tpu as pltpu
from jax.sharding import PartitionSpec as P

clip_rms = 0.5
momentum_decay = 0.9
step_rate = 0.5
VMEM = pltpu.VMEM
PARTS = 6
CHUNKS = 2
ZHEAD = 5
NN = (((1,), (0,)), ((), ()))
NT = (((1,), (1,)), ((), ()))


def split_table(table):
    high = table.astype(ml_dtypes.bfloat16)
    low = (table - high.astype(np.float64)).astype(ml_dtypes.bfloat16)
    return high, low


def tables():
    u = np.arange(64, dtype=np.float64)[:, None]
    x = np.arange(64, dtype=np.float64)[None, :]
    weight = np.where(u == 0, np.sqrt(1.0 / 64.0), np.sqrt(2.0 / 64.0))
    dct = weight * np.cos(np.pi * (2.0 * x + 1.0) * u / 128.0)
    pair = np.kron(np.eye(2), dct)
    rows = np.zeros((2, 64, 2, 2, 32))
    by_parity = dct.reshape(32, 2, 64)
    for i in range(2):
        rows[i, :, :, i, :] = by_parity.transpose(2, 1, 0)
    return pair, rows.reshape(128, 128)


def widen(table):
    high, low = split_table(table)
    return np.block([[high, high], [low, low]])


def split(value):
    high = value.astype(jnp.bfloat16)
    low = (value - high.astype(jnp.float32)).astype(jnp.bfloat16)
    return high, low


def dot(left, right, dims):
    return lax.dot_general(left, right, dims, preferred_element_type=jnp.float32)


def duplicate(packed):
    lane = lax.broadcasted_iota(jnp.int32, packed.shape, 1)
    other = pltpu.roll(packed, 64, 1)
    return jnp.where(lane < 64, packed, other), jnp.where(lane < 64, other, packed)


def block(k):
    return pl.ds(k * 128 if isinstance(k, int) else pl.multiple_of(k * 128, 128), 128)


def row(k, groups):
    return pl.ds((k % 2) * (groups // 2) + k // 2, 1)


def in_hbm(*arrays):
    return [pltpu.with_memory_space_constraint(array, pltpu.HBM) for array in arrays]


def put_split(ref, value):
    high, low = split(value)
    for n in range(value.shape[1] // 128):
        ref[n * 128 : (n + 1) * 128, :128] = high[:, n * 128 : (n + 1) * 128]
        ref[n * 128 : (n + 1) * 128, 128:] = low[:, n * 128 : (n + 1) * 128]


def fetch_kernel(grad_hbm, *refs):
    count = (len(refs) - 4) // 2
    sources, out_hbm, grad_ref = refs[:count], refs[count], refs[count + 1]
    targets, out_ref, sems = refs[count + 2 : -2], refs[-2], refs[-1]
    width = grad_ref.shape[1] // CHUNKS
    copies = [
        pltpu.make_async_copy(
            grad_hbm.at[:, pl.ds(n * width, width)],
            grad_ref.at[:, pl.ds(n * width, width)],
            sems.at[n],
        )
        for n in range(CHUNKS)
    ]
    copies += [
        pltpu.make_async_copy(source, target, sems.at[CHUNKS + n])
        for n, (source, target) in enumerate(zip(sources, targets))
    ]
    for copy in copies:
        copy.start()
    total = jnp.zeros((8, 128), jnp.float32)
    for n in range(CHUNKS):
        copies[n].wait()
        for k in range(n * width // 128, (n + 1) * width // 128):
            value = grad_ref[:, block(k)].astype(jnp.float32)
            total = total + jnp.sum((value * value).reshape(-1, 8, 128), axis=0)
    out_ref[...] = jnp.broadcast_to(
        jnp.sum(total, axis=0, keepdims=True)[None], out_ref.shape
    )
    copies.append(pltpu.make_async_copy(out_ref, out_hbm, sems.at[len(copies)]))
    copies[-1].start()
    for copy in copies[CHUNKS:]:
        copy.wait()


def pick_kernel(
    kept_ref, grad_ref, moment_ref, forth_ref, pair_ref, out_ref, listed_ref, at_ref, first_ref, picked_ref
):
    groups = out_ref.shape[1]
    half = groups // 2
    lane = lax.broadcasted_iota(jnp.int32, (half, 128), 1)
    for i in range(2):
        for n in range(half):
            listed_ref[i, n : n + 1] = kept_ref[i : i + 1, n * 128 : (n + 1) * 128]
    offsets = [(listed_ref[i] & 127).astype(jnp.float32) for i in range(2)]
    for q in range(2):
        placed = []
        for h in range(2):
            here = (2 * q + h) * 32
            front = pltpu.roll(offsets[0], (128 - here) % 128, 1)
            back = pltpu.roll(offsets[1], (160 - here) % 128, 1)
            placed.append(jnp.where(lane < 32, front, back))
            there = pltpu.roll(placed[h], 64, 1)
            at_ref[h, q * half : (q + 1) * half] = jnp.where(lane < 64, placed[h], there - 64.0)
        out_ref[2, q * half : (q + 1) * half] = jnp.where(
            lane < 64, placed[0], pltpu.roll(placed[1], 64, 1)
        )
    level = lax.broadcasted_iota(jnp.int32, (64, 128), 0).astype(jnp.float32)

    def over_rows(k):
        both = jnp.concatenate([grad_ref[:, block(k)], moment_ref[:, block(k)]], axis=1)
        twice = jnp.concatenate([both, both], axis=0)
        put_split(first_ref.at[k], dot(forth_ref[...], twice, NN))

    def over_columns(k):
        coeffs = dot(pair_ref[...], first_ref[k], NT)
        coeffs = coeffs[:128] + coeffs[128:]
        for h in range(2):
            hit = level == at_ref[h, row(k, groups), :]
            for n in range(2):
                part = coeffs[h * 64 : (h + 1) * 64, n * 128 : (n + 1) * 128]
                picked_ref[n, h, row(k, groups), :] = jnp.sum(
                    jnp.where(hit, part, 0.0), axis=0, keepdims=True
                )

    for step in (over_rows, over_columns):
        for k in range(groups):
            step(k)
    lane = lax.broadcasted_iota(jnp.int32, (groups, 128), 1)
    for n in range(2):
        front, back = picked_ref[n, 0], picked_ref[n, 1]
        front = front + pltpu.roll(front, 64, 1)
        back = back + pltpu.roll(back, 64, 1)
        out_ref[n] = jnp.where(lane < 64, front, back)


def scale_kernel(count, squares_ref, picked_ref, factor_ref, own_ref, send_ref):
    total = jnp.sum(jnp.sum(squares_ref[...], axis=0), axis=1, keepdims=True)
    mean_square = jnp.broadcast_to(total, (1, 128)) / count
    factor = jnp.minimum(1.0, clip_rms / jnp.sqrt(mean_square + 1e-06))
    factor_ref[...] = factor
    values = momentum_decay * picked_ref[1] + factor * picked_ref[0]
    listing = jnp.concatenate([values, picked_ref[2]], axis=0)
    own_ref[...] = listing
    send_ref[...] = jnp.broadcast_to(listing[None], send_ref.shape)


def unpack(listings, at_ref, value_ref):
    groups = at_ref.shape[2]
    lane = lax.broadcasted_iota(jnp.int32, (groups, 128), 1)
    offsets = [listing[groups:] for listing in listings]
    for r in range(len(listings)):
        total = listings[r][:groups]
        for s in range(r):
            total = total + jnp.where(offsets[s] == offsets[r], listings[s][:groups], 0.0)
        values = duplicate(total)
        for h, offset in enumerate(duplicate(offsets[r])):
            value_ref[r, h] = values[h]
            at_ref[r, h] = jnp.where(lane < 64, offset, offset - 64.0)


def decode(at_ref, value_ref, sparse_ref, second_ref, back_ref, tall_ref, ready, emit):
    lists, _, groups, _ = at_ref.shape
    level = lax.broadcasted_iota(jnp.int32, (64, 128), 0).astype(jnp.float32)

    def scatter(t, carry):
        for k in range(2):
            for h in range(2):
                part = jnp.zeros((64, 128), jnp.float32)
                for r in range(lists):
                    hit = level == at_ref[r, h, row(2 * t + k, groups), :]
                    part = jnp.where(hit, value_ref[r, h, row(2 * t + k, groups), :], part)
                high, low = split(part)
                at = slice(k * 128 + h * 64, k * 128 + h * 64 + 64)
                sparse_ref[t, at, :128] = high
                sparse_ref[t, at, 128:] = low
        return carry

    lax.fori_loop(0, groups // 2, scatter, 0, unroll=3 if groups % 6 == 0 else 1)
    for copy in ready:
        copy.wait()
    for t in range(groups // 2):
        first = dot(back_ref[...], sparse_ref[t], NT)
        put_split(second_ref.at[t], first[:128] + first[128:])
    for t in range(groups // 2):
        decoded = dot(second_ref[t], tall_ref[...], NN)
        decoded = decoded[:, :128] + decoded[:, 128:]
        for k in range(2):
            emit(2 * t + k, decoded[k * 128 : (k + 1) * 128])


def fetch(sems, *pairs):
    copies = [pltpu.make_async_copy(source, target, sems.at[n]) for n, (source, target) in enumerate(pairs)]
    for copy in copies:
        copy.start()
    return copies


class Outlet:
    def __init__(self, source, target, sems, first_sem):
        self.source, self.target, self.sems, self.first_sem = source, target, sems, first_sem
        self.per = max(2, source.shape[1] // 128 // PARTS)
        self.copies = []

    def put(self, k, value):
        self.source[:, block(k)] = value.astype(self.source.dtype)
        if (k + 1) % self.per == 0:
            at = pl.ds((k + 1 - self.per) * 128, self.per * 128)
            copy = pltpu.make_async_copy(
                self.source.at[:, at],
                self.target.at[:, at],
                self.sems.at[self.first_sem + len(self.copies)],
            )
            copy.start()
            self.copies.append(copy)

    def wait(self):
        for copy in self.copies:
            copy.wait()


def own_kernel(
    own_ref, factor_ref, grad_ref, moment_ref, back_hbm, tall_hbm, new_moment_hbm,
    back_ref, tall_ref, at_ref, value_ref, sparse_ref, second_ref, out_ref, sems,
):
    ready = fetch(sems, (back_hbm, back_ref), (tall_hbm, tall_ref))
    factor = factor_ref[...]
    unpack([own_ref[...]], at_ref, value_ref)
    outlet = Outlet(out_ref, new_moment_hbm, sems, 2)

    def emit(k, decoded):
        blended = momentum_decay * moment_ref[:, block(k)].astype(jnp.float32)
        blended = blended + factor * grad_ref[:, block(k)].astype(jnp.float32)
        outlet.put(k, blended - decoded)

    decode(at_ref, value_ref, sparse_ref, second_ref, back_ref, tall_ref, ready, emit)
    outlet.wait()


def finish_kernel(
    all_ref, back_hbm, tall_hbm, weight_hbm, new_weight_hbm,
    back_ref, tall_ref, weight_ref, at_ref, value_ref, sparse_ref, second_ref, out_ref, sems,
):
    ready = fetch(sems, (back_hbm, back_ref), (tall_hbm, tall_ref), (weight_hbm, weight_ref))
    unpack([all_ref[r] for r in range(all_ref.shape[0])], at_ref, value_ref)
    outlet = Outlet(out_ref, new_weight_hbm, sems, 3)

    def emit(k, decoded):
        outlet.put(k, weight_ref[:, block(k)].astype(jnp.float32) - step_rate * decoded)

    decode(at_ref, value_ref, sparse_ref, second_ref, back_ref, tall_ref, ready, emit)
    outlet.wait()


def ring_order(size):
    head = size // 2 + 2 if size == 32 else 0
    return [head] + [member for member in range(size) if member != head]


def chip_order(size):
    head = ZHEAD % size
    return [(head - n) % size for n in range(size)]


def body(grad, momentum, kept_index, weights):
    grad, momentum = grad[0], momentum[0]
    rows, cols = grad.shape
    ring = lax.axis_size("fsdp")
    replicas = lax.axis_size("rep")
    groups = cols // 128
    bf16, f32 = jnp.bfloat16, jnp.float32
    pair, back = tables()
    forth = jnp.asarray(np.concatenate(split_table(back.T), axis=1))
    back_wide = jnp.asarray(widen(back))
    pair_wide = jnp.asarray(widen(pair))
    pair_tall = jnp.asarray(np.ascontiguousarray(widen(pair.T).T))
    whole = pl.BlockSpec(memory_space=VMEM)
    hbm = pl.BlockSpec(memory_space=pl.ANY)
    params = pltpu.CompilerParams(vmem_limit_bytes=32 * 1024 * 1024)
    full = jax.ShapeDtypeStruct((rows, cols), bf16)
    square = jax.ShapeDtypeStruct((256, 256), bf16)

    squares, grad_near, moment_near, kept_near, forth_near, pair_near = pl.pallas_call(
        fetch_kernel,
        out_shape=(
            jax.ShapeDtypeStruct((ring, 1, 128), f32),
            full,
            full,
            jax.ShapeDtypeStruct(kept_index.shape[1:], jnp.int32),
            jax.ShapeDtypeStruct((128, 256), bf16),
            square,
        ),
        in_specs=[hbm] * 5,
        out_specs=(hbm,) + (whole,) * 5,
        scratch_shapes=[VMEM((ring, 1, 128), f32), pltpu.SemaphoreType.DMA((CHUNKS + 5,))],
        compiler_params=params,
        name="fetch",
    )(*in_hbm(grad, momentum, kept_index[0], forth, pair_wide))
    squares = lax.all_to_all(
        squares, "fsdp", 0, 0, tiled=True, axis_index_groups=[ring_order(ring)]
    )

    picked = pl.pallas_call(
        pick_kernel,
        out_shape=jax.ShapeDtypeStruct((3, groups, 128), f32),
        in_specs=[whole] * 5,
        out_specs=whole,
        scratch_shapes=[
            VMEM((2, groups // 2, 128), jnp.int32),
            VMEM((2, groups, 128), f32),
            VMEM((groups, 256, 256), bf16),
            VMEM((2, 2, groups, 128), f32),
        ],
        compiler_params=params,
        cost_estimate=pl.CostEstimate(
            flops=2 * 2 * 10 * 128 * 128 * cols, bytes_accessed=4 * rows * cols, transcendentals=0
        ),
        name="pick",
    )(kept_near, grad_near, moment_near, forth_near, pair_near)

    factor, own, send = pl.pallas_call(
        functools.partial(scale_kernel, float(rows * ring * cols)),
        out_shape=(
            jax.ShapeDtypeStruct((1, 128), f32),
            jax.ShapeDtypeStruct((2 * groups, 128), f32),
            jax.ShapeDtypeStruct((replicas // 2, 2 * groups, 128), f32),
        ),
        in_specs=[whole] * 2,
        out_specs=(whole,) * 3,
        compiler_params=params,
        name="scale",
    )(squares, picked)

    by_core = [[chip * 2 + core for chip in chip_order(replicas // 2)] for core in range(2)]
    every = lax.all_to_all(send, "rep", 0, 0, tiled=True, axis_index_groups=by_core)
    cores = [[chip * 2 + core for core in range(2)] for chip in range(replicas // 2)]
    every = lax.all_gather(every, "rep", axis=0, tiled=True, axis_index_groups=cores)

    def work(lists):
        return [
            VMEM((lists, 2, groups, 128), f32),
            VMEM((lists, 2, groups, 128), f32),
            VMEM((groups // 2, 256, 256), bf16),
            VMEM((groups // 2, 256, 256), bf16),
            VMEM((rows, cols), bf16),
            pltpu.SemaphoreType.DMA((3 + groups // 2,)),
        ]

    new_momentum = pl.pallas_call(
        own_kernel,
        out_shape=full,
        in_specs=[whole] * 4 + [hbm] * 2,
        out_specs=hbm,
        scratch_shapes=[VMEM((256, 256), bf16)] * 2 + work(1),
        compiler_params=params,
        cost_estimate=pl.CostEstimate(
            flops=2 * 2 * 10 * 128 * 128 * cols, bytes_accessed=4 * rows * cols, transcendentals=0
        ),
        name="own",
    )(own, factor, grad_near, moment_near, *in_hbm(back_wide, pair_tall))

    new_weights = pl.pallas_call(
        finish_kernel,
        out_shape=full,
        in_specs=[whole] + [hbm] * 3,
        out_specs=hbm,
        scratch_shapes=[VMEM((256, 256), bf16)] * 2 + [VMEM((rows, cols), bf16)] + work(replicas),
        compiler_params=params,
        name="finish",
    )(every, *in_hbm(back_wide, pair_tall, weights))
    return (new_momentum[None], new_weights)


def solution(mesh):
    in_specs = (
        P("rep", "fsdp", None),
        P("rep", "fsdp", None),
        P("rep", "fsdp", None),
        P("fsdp", None),
    )
    out_specs = (P("rep", "fsdp", None), P("fsdp", None))
    return jax.shard_map(body, mesh=mesh, in_specs=in_specs, out_specs=out_specs, check_vma=False)
```

```python
import functools

import jax
import jax.numpy as jnp
import ml_dtypes
import numpy as np
from jax import lax
from jax.experimental import pallas as pl
from jax.experimental.pallas import tpu as pltpu
from jax.sharding import PartitionSpec as P

clip_rms = 0.5
momentum_decay = 0.9
step_rate = 0.5
VMEM = pltpu.VMEM
PARTS = 6
CHUNKS = 2
NN = (((1,), (0,)), ((), ()))
NT = (((1,), (1,)), ((), ()))


def split_table(table):
    high = table.astype(ml_dtypes.bfloat16)
    low = (table - high.astype(np.float64)).astype(ml_dtypes.bfloat16)
    return high, low


def tables():
    u = np.arange(64, dtype=np.float64)[:, None]
    x = np.arange(64, dtype=np.float64)[None, :]
    weight = np.where(u == 0, np.sqrt(1.0 / 64.0), np.sqrt(2.0 / 64.0))
    dct = weight * np.cos(np.pi * (2.0 * x + 1.0) * u / 128.0)
    pair = np.kron(np.eye(2), dct)
    rows = np.zeros((2, 64, 2, 2, 32))
    by_parity = dct.reshape(32, 2, 64)
    for i in range(2):
        rows[i, :, :, i, :] = by_parity.transpose(2, 1, 0)
    return pair, rows.reshape(128, 128)


def widen(table):
    high, low = split_table(table)
    return np.block([[high, high], [low, low]])


def split(value):
    high = value.astype(jnp.bfloat16)
    low = (value - high.astype(jnp.float32)).astype(jnp.bfloat16)
    return high, low


def dot(left, right, dims):
    return lax.dot_general(left, right, dims, preferred_element_type=jnp.float32)


def duplicate(packed):
    lane = lax.broadcasted_iota(jnp.int32, packed.shape, 1)
    other = pltpu.roll(packed, 64, 1)
    return jnp.where(lane < 64, packed, other), jnp.where(lane < 64, other, packed)


def block(k):
    return pl.ds(k * 128 if isinstance(k, int) else pl.multiple_of(k * 128, 128), 128)


def row(k, groups):
    return pl.ds((k % 2) * (groups // 2) + k // 2, 1)


def in_hbm(*arrays):
    return [pltpu.with_memory_space_constraint(array, pltpu.HBM) for array in arrays]


def put_split(ref, value):
    high, low = split(value)
    for n in range(value.shape[1] // 128):
        ref[n * 128 : (n + 1) * 128, :128] = high[:, n * 128 : (n + 1) * 128]
        ref[n * 128 : (n + 1) * 128, 128:] = low[:, n * 128 : (n + 1) * 128]


def fetch_kernel(grad_hbm, *refs):
    count = (len(refs) - 4) // 2
    sources, out_hbm, grad_ref = refs[:count], refs[count], refs[count + 1]
    targets, out_ref, sems = refs[count + 2 : -2], refs[-2], refs[-1]
    width = grad_ref.shape[1] // CHUNKS
    copies = [
        pltpu.make_async_copy(
            grad_hbm.at[:, pl.ds(n * width, width)],
            grad_ref.at[:, pl.ds(n * width, width)],
            sems.at[n],
        )
        for n in range(CHUNKS)
    ]
    copies += [
        pltpu.make_async_copy(source, target, sems.at[CHUNKS + n])
        for n, (source, target) in enumerate(zip(sources, targets))
    ]
    for copy in copies:
        copy.start()
    total = jnp.zeros((8, 128), jnp.float32)
    for n in range(CHUNKS):
        copies[n].wait()
        for k in range(n * width // 128, (n + 1) * width // 128):
            value = grad_ref[:, block(k)].astype(jnp.float32)
            total = total + jnp.sum((value * value).reshape(-1, 8, 128), axis=0)
    out_ref[...] = jnp.broadcast_to(
        jnp.sum(total, axis=0, keepdims=True)[None], out_ref.shape
    )
    copies.append(pltpu.make_async_copy(out_ref, out_hbm, sems.at[len(copies)]))
    copies[-1].start()
    for copy in copies[CHUNKS:]:
        copy.wait()


def pick_kernel(
    kept_ref, grad_ref, moment_ref, forth_ref, pair_ref, out_ref, listed_ref, at_ref, first_ref, picked_ref
):
    groups = out_ref.shape[1]
    half = groups // 2
    lane = lax.broadcasted_iota(jnp.int32, (half, 128), 1)
    for i in range(2):
        for n in range(half):
            listed_ref[i, n : n + 1] = kept_ref[i : i + 1, n * 128 : (n + 1) * 128]
    offsets = [(listed_ref[i] & 127).astype(jnp.float32) for i in range(2)]
    for q in range(2):
        placed = []
        for h in range(2):
            here = (2 * q + h) * 32
            front = pltpu.roll(offsets[0], (128 - here) % 128, 1)
            back = pltpu.roll(offsets[1], (160 - here) % 128, 1)
            placed.append(jnp.where(lane < 32, front, back))
            there = pltpu.roll(placed[h], 64, 1)
            at_ref[h, q * half : (q + 1) * half] = jnp.where(lane < 64, placed[h], there - 64.0)
        out_ref[2, q * half : (q + 1) * half] = jnp.where(
            lane < 64, placed[0], pltpu.roll(placed[1], 64, 1)
        )
    level = lax.broadcasted_iota(jnp.int32, (64, 128), 0).astype(jnp.float32)

    def over_rows(k):
        both = jnp.concatenate([grad_ref[:, block(k)], moment_ref[:, block(k)]], axis=1)
        twice = jnp.concatenate([both, both], axis=0)
        put_split(first_ref.at[k], dot(forth_ref[...], twice, NN))

    def over_columns(k):
        coeffs = dot(pair_ref[...], first_ref[k], NT)
        coeffs = coeffs[:128] + coeffs[128:]
        for h in range(2):
            hit = level == at_ref[h, row(k, groups), :]
            for n in range(2):
                part = coeffs[h * 64 : (h + 1) * 64, n * 128 : (n + 1) * 128]
                picked_ref[n, h, row(k, groups), :] = jnp.sum(
                    jnp.where(hit, part, 0.0), axis=0, keepdims=True
                )

    for step in (over_rows, over_columns):
        for k in range(groups):
            step(k)
    lane = lax.broadcasted_iota(jnp.int32, (groups, 128), 1)
    for n in range(2):
        front, back = picked_ref[n, 0], picked_ref[n, 1]
        front = front + pltpu.roll(front, 64, 1)
        back = back + pltpu.roll(back, 64, 1)
        out_ref[n] = jnp.where(lane < 64, front, back)


def scale_kernel(count, squares_ref, picked_ref, factor_ref, own_ref, send_ref):
    total = jnp.sum(jnp.sum(squares_ref[...], axis=0), axis=1, keepdims=True)
    mean_square = jnp.broadcast_to(total, (1, 128)) / count
    factor = jnp.minimum(1.0, clip_rms / jnp.sqrt(mean_square + 1e-06))
    factor_ref[...] = factor
    values = momentum_decay * picked_ref[1] + factor * picked_ref[0]
    listing = jnp.concatenate([values, picked_ref[2]], axis=0)
    own_ref[...] = listing
    send_ref[...] = jnp.broadcast_to(listing[None], send_ref.shape)


def unpack(listings, at_ref, value_ref):
    groups = at_ref.shape[2]
    lane = lax.broadcasted_iota(jnp.int32, (groups, 128), 1)
    offsets = [listing[groups:] for listing in listings]
    for r in range(len(listings)):
        total = listings[r][:groups]
        for s in range(r):
            total = total + jnp.where(offsets[s] == offsets[r], listings[s][:groups], 0.0)
        values = duplicate(total)
        for h, offset in enumerate(duplicate(offsets[r])):
            value_ref[r, h] = values[h]
            at_ref[r, h] = jnp.where(lane < 64, offset, offset - 64.0)


def decode(at_ref, value_ref, sparse_ref, second_ref, back_ref, tall_ref, ready, emit):
    lists, _, groups, _ = at_ref.shape
    level = lax.broadcasted_iota(jnp.int32, (64, 128), 0).astype(jnp.float32)

    def scatter(t, carry):
        for k in range(2):
            for h in range(2):
                part = jnp.zeros((64, 128), jnp.float32)
                for r in range(lists):
                    hit = level == at_ref[r, h, row(2 * t + k, groups), :]
                    part = jnp.where(hit, value_ref[r, h, row(2 * t + k, groups), :], part)
                high, low = split(part)
                at = slice(k * 128 + h * 64, k * 128 + h * 64 + 64)
                sparse_ref[t, at, :128] = high
                sparse_ref[t, at, 128:] = low
        return carry

    lax.fori_loop(0, groups // 2, scatter, 0, unroll=3 if groups % 6 == 0 else 1)
    for copy in ready:
        copy.wait()
    for t in range(groups // 2):
        first = dot(back_ref[...], sparse_ref[t], NT)
        put_split(second_ref.at[t], first[:128] + first[128:])
    for t in range(groups // 2):
        decoded = dot(second_ref[t], tall_ref[...], NN)
        decoded = decoded[:, :128] + decoded[:, 128:]
        for k in range(2):
            emit(2 * t + k, decoded[k * 128 : (k + 1) * 128])


def fetch(sems, *pairs):
    copies = [pltpu.make_async_copy(source, target, sems.at[n]) for n, (source, target) in enumerate(pairs)]
    for copy in copies:
        copy.start()
    return copies


class Outlet:
    def __init__(self, source, target, sems, first_sem):
        self.source, self.target, self.sems, self.first_sem = source, target, sems, first_sem
        self.per = max(2, source.shape[1] // 128 // PARTS)
        self.copies = []

    def put(self, k, value):
        self.source[:, block(k)] = value.astype(self.source.dtype)
        if (k + 1) % self.per == 0:
            at = pl.ds((k + 1 - self.per) * 128, self.per * 128)
            copy = pltpu.make_async_copy(
                self.source.at[:, at],
                self.target.at[:, at],
                self.sems.at[self.first_sem + len(self.copies)],
            )
            copy.start()
            self.copies.append(copy)

    def wait(self):
        for copy in self.copies:
            copy.wait()


def own_kernel(
    own_ref, factor_ref, grad_ref, moment_ref, back_hbm, tall_hbm, new_moment_hbm,
    back_ref, tall_ref, at_ref, value_ref, sparse_ref, second_ref, out_ref, sems,
):
    ready = fetch(sems, (back_hbm, back_ref), (tall_hbm, tall_ref))
    factor = factor_ref[...]
    unpack([own_ref[...]], at_ref, value_ref)
    outlet = Outlet(out_ref, new_moment_hbm, sems, 2)

    def emit(k, decoded):
        blended = momentum_decay * moment_ref[:, block(k)].astype(jnp.float32)
        blended = blended + factor * grad_ref[:, block(k)].astype(jnp.float32)
        outlet.put(k, blended - decoded)

    decode(at_ref, value_ref, sparse_ref, second_ref, back_ref, tall_ref, ready, emit)
    outlet.wait()


def finish_kernel(
    all_ref, back_hbm, tall_hbm, weight_hbm, new_weight_hbm,
    back_ref, tall_ref, weight_ref, at_ref, value_ref, sparse_ref, second_ref, out_ref, sems,
):
    ready = fetch(sems, (back_hbm, back_ref), (tall_hbm, tall_ref), (weight_hbm, weight_ref))
    unpack([all_ref[r] for r in range(all_ref.shape[0])], at_ref, value_ref)
    outlet = Outlet(out_ref, new_weight_hbm, sems, 3)

    def emit(k, decoded):
        outlet.put(k, weight_ref[:, block(k)].astype(jnp.float32) - step_rate * decoded)

    decode(at_ref, value_ref, sparse_ref, second_ref, back_ref, tall_ref, ready, emit)
    outlet.wait()


def led_by(head, members):
    return [head] + [member for member in members if member != head]


def ring_groups(replicas, size):
    heads = (18, 22) if size == 32 else (0, 0)
    return [
        [r * size + member for member in led_by(heads[r % 2], range(size))] for r in range(replicas)
    ]


def chip_groups(replicas):
    chips = replicas // 2
    return [
        [(head - n) % chips * 2 + core for n in range(chips)] for core, head in enumerate((5, 6))
    ]


def body(grad, momentum, kept_index, weights):
    grad, momentum = grad[0], momentum[0]
    rows, cols = grad.shape
    ring = lax.axis_size("fsdp")
    replicas = lax.axis_size("rep")
    groups = cols // 128
    bf16, f32 = jnp.bfloat16, jnp.float32
    pair, back = tables()
    forth = jnp.asarray(np.concatenate(split_table(back.T), axis=1))
    back_wide = jnp.asarray(widen(back))
    pair_wide = jnp.asarray(widen(pair))
    pair_tall = jnp.asarray(np.ascontiguousarray(widen(pair.T).T))
    whole = pl.BlockSpec(memory_space=VMEM)
    hbm = pl.BlockSpec(memory_space=pl.ANY)
    params = pltpu.CompilerParams(vmem_limit_bytes=32 * 1024 * 1024)
    full = jax.ShapeDtypeStruct((rows, cols), bf16)
    square = jax.ShapeDtypeStruct((256, 256), bf16)

    squares, grad_near, moment_near, kept_near, forth_near, pair_near = pl.pallas_call(
        fetch_kernel,
        out_shape=(
            jax.ShapeDtypeStruct((ring, 1, 128), f32),
            full,
            full,
            jax.ShapeDtypeStruct(kept_index.shape[1:], jnp.int32),
            jax.ShapeDtypeStruct((128, 256), bf16),
            square,
        ),
        in_specs=[hbm] * 5,
        out_specs=(hbm,) + (whole,) * 5,
        scratch_shapes=[VMEM((ring, 1, 128), f32), pltpu.SemaphoreType.DMA((CHUNKS + 5,))],
        compiler_params=params,
        name="fetch",
    )(*in_hbm(grad, momentum, kept_index[0], forth, pair_wide))
    squares = lax.all_to_all(
        squares,
        ("rep", "fsdp"),
        0,
        0,
        tiled=True,
        axis_index_groups=ring_groups(replicas, ring),
    )

    picked = pl.pallas_call(
        pick_kernel,
        out_shape=jax.ShapeDtypeStruct((3, groups, 128), f32),
        in_specs=[whole] * 5,
        out_specs=whole,
        scratch_shapes=[
            VMEM((2, groups // 2, 128), jnp.int32),
            VMEM((2, groups, 128), f32),
            VMEM((groups, 256, 256), bf16),
            VMEM((2, 2, groups, 128), f32),
        ],
        compiler_params=params,
        cost_estimate=pl.CostEstimate(
            flops=2 * 2 * 10 * 128 * 128 * cols, bytes_accessed=4 * rows * cols, transcendentals=0
        ),
        name="pick",
    )(kept_near, grad_near, moment_near, forth_near, pair_near)

    factor, own, send = pl.pallas_call(
        functools.partial(scale_kernel, float(rows * ring * cols)),
        out_shape=(
            jax.ShapeDtypeStruct((1, 128), f32),
            jax.ShapeDtypeStruct((2 * groups, 128), f32),
            jax.ShapeDtypeStruct((replicas // 2, 2 * groups, 128), f32),
        ),
        in_specs=[whole] * 2,
        out_specs=(whole,) * 3,
        compiler_params=params,
        name="scale",
    )(squares, picked)

    every = lax.all_to_all(
        send, "rep", 0, 0, tiled=True, axis_index_groups=chip_groups(replicas)
    )
    cores = [[chip * 2 + core for core in range(2)] for chip in range(replicas // 2)]
    every = lax.all_gather(every, "rep", axis=0, tiled=True, axis_index_groups=cores)

    def work(lists):
        return [
            VMEM((lists, 2, groups, 128), f32),
            VMEM((lists, 2, groups, 128), f32),
            VMEM((groups // 2, 256, 256), bf16),
            VMEM((groups // 2, 256, 256), bf16),
            VMEM((rows, cols), bf16),
            pltpu.SemaphoreType.DMA((3 + groups // 2,)),
        ]

    new_momentum = pl.pallas_call(
        own_kernel,
        out_shape=full,
        in_specs=[whole] * 4 + [hbm] * 2,
        out_specs=hbm,
        scratch_shapes=[VMEM((256, 256), bf16)] * 2 + work(1),
        compiler_params=params,
        cost_estimate=pl.CostEstimate(
            flops=2 * 2 * 10 * 128 * 128 * cols, bytes_accessed=4 * rows * cols, transcendentals=0
        ),
        name="own",
    )(own, factor, grad_near, moment_near, *in_hbm(back_wide, pair_tall))

    new_weights = pl.pallas_call(
        finish_kernel,
        out_shape=full,
        in_specs=[whole] + [hbm] * 3,
        out_specs=hbm,
        scratch_shapes=[VMEM((256, 256), bf16)] * 2 + [VMEM((rows, cols), bf16)] + work(replicas),
        compiler_params=params,
        name="finish",
    )(every, *in_hbm(back_wide, pair_tall, weights))
    return (new_momentum[None], new_weights)


def solution(mesh):
    in_specs = (
        P("rep", "fsdp", None),
        P("rep", "fsdp", None),
        P("rep", "fsdp", None),
        P("fsdp", None),
    )
    out_specs = (P("rep", "fsdp", None), P("fsdp", None))
    return jax.shard_map(body, mesh=mesh, in_specs=in_specs, out_specs=out_specs, check_vma=False)
```

```python
import functools

import jax
import jax.numpy as jnp
import ml_dtypes
import numpy as np
from jax import lax
from jax.experimental import pallas as pl
from jax.experimental.pallas import tpu as pltpu
from jax.sharding import PartitionSpec as P

clip_rms = 0.5
momentum_decay = 0.9
step_rate = 0.5
VMEM = pltpu.VMEM
SPARE = 8
PARTS = 6
CHUNKS = 2
NN = (((1,), (0,)), ((), ()))
NT = (((1,), (1,)), ((), ()))


def split_table(table):
    high = table.astype(ml_dtypes.bfloat16)
    low = (table - high.astype(np.float64)).astype(ml_dtypes.bfloat16)
    return high, low


def tables():
    u = np.arange(64, dtype=np.float64)[:, None]
    x = np.arange(64, dtype=np.float64)[None, :]
    weight = np.where(u == 0, np.sqrt(1.0 / 64.0), np.sqrt(2.0 / 64.0))
    dct = weight * np.cos(np.pi * (2.0 * x + 1.0) * u / 128.0)
    pair = np.kron(np.eye(2), dct)
    rows = np.zeros((2, 64, 2, 2, 32))
    by_parity = dct.reshape(32, 2, 64)
    for i in range(2):
        rows[i, :, :, i, :] = by_parity.transpose(2, 1, 0)
    return pair, rows.reshape(128, 128)


def widen(table):
    high, low = split_table(table)
    return np.block([[high, high], [low, low]])


def split(value):
    high = value.astype(jnp.bfloat16)
    low = (value - high.astype(jnp.float32)).astype(jnp.bfloat16)
    return high, low


def dot(left, right, dims):
    return lax.dot_general(left, right, dims, preferred_element_type=jnp.float32)


def duplicate(packed):
    lane = lax.broadcasted_iota(jnp.int32, packed.shape, 1)
    other = pltpu.roll(packed, 64, 1)
    return jnp.where(lane < 64, packed, other), jnp.where(lane < 64, other, packed)


def block(k):
    return pl.ds(k * 128 if isinstance(k, int) else pl.multiple_of(k * 128, 128), 128)


def row(k, groups):
    return pl.ds((k % 2) * (groups // 2) + k // 2, 1)


def in_hbm(*arrays):
    return [pltpu.with_memory_space_constraint(array, pltpu.HBM) for array in arrays]


def put_split(ref, value):
    high, low = split(value)
    for n in range(value.shape[1] // 128):
        ref[n * 128 : (n + 1) * 128, :128] = high[:, n * 128 : (n + 1) * 128]
        ref[n * 128 : (n + 1) * 128, 128:] = low[:, n * 128 : (n + 1) * 128]


def fetch_kernel(grad_hbm, *refs):
    count = (len(refs) - 4) // 2
    sources, out_hbm, grad_ref = refs[:count], refs[count], refs[count + 1]
    targets, out_ref, sems = refs[count + 2 : -2], refs[-2], refs[-1]
    width = grad_ref.shape[1] // CHUNKS
    copies = [
        pltpu.make_async_copy(
            grad_hbm.at[:, pl.ds(n * width, width)],
            grad_ref.at[:, pl.ds(n * width, width)],
            sems.at[n],
        )
        for n in range(CHUNKS)
    ]
    copies += [
        pltpu.make_async_copy(source, target, sems.at[CHUNKS + n])
        for n, (source, target) in enumerate(zip(sources, targets))
    ]
    for copy in copies:
        copy.start()
    total = jnp.zeros((8, 128), jnp.float32)
    for n in range(CHUNKS):
        copies[n].wait()
        for k in range(n * width // 128, (n + 1) * width // 128):
            value = grad_ref[:, block(k)].astype(jnp.float32)
            total = total + jnp.sum((value * value).reshape(-1, 8, 128), axis=0)
    out_ref[...] = jnp.broadcast_to(
        jnp.sum(total, axis=0, keepdims=True)[None], out_ref.shape
    )
    copies.append(pltpu.make_async_copy(out_ref, out_hbm, sems.at[len(copies)]))
    copies[-1].start()
    for copy in copies[CHUNKS:]:
        copy.wait()


def pick_kernel(
    kept_ref, grad_ref, moment_ref, forth_ref, pair_ref, out_ref, listed_ref, at_ref, placed_ref, first_ref, picked_ref
):
    groups = out_ref.shape[1]
    half = groups // 2
    lane = lax.broadcasted_iota(jnp.int32, (half, 128), 1)
    kept = kept_ref[...]
    for i in range(2):
        for n in range(half):
            listed_ref[i, n : n + 1] = kept[i : i + 1, n * 128 : (n + 1) * 128]
    offsets = [(listed_ref[i, :half] & 127).astype(jnp.float32) for i in range(2)]
    for q in range(2):
        placed = []
        for h in range(2):
            here = (2 * q + h) * 32
            front = pltpu.roll(offsets[0], (128 - here) % 128, 1)
            back = pltpu.roll(offsets[1], (160 - here) % 128, 1)
            placed.append(jnp.where(lane < 32, front, back))
            there = pltpu.roll(placed[h], 64, 1)
            at_ref[h, q * half : (q + 1) * half] = jnp.where(lane < 64, placed[h], there - 64.0)
        placed_ref[q * half : (q + 1) * half] = jnp.where(
            lane < 64, placed[0], pltpu.roll(placed[1], 64, 1)
        )
    out_ref[2] = placed_ref[:groups]
    level = lax.broadcasted_iota(jnp.int32, (64, 128), 0).astype(jnp.float32)

    def over_rows(k):
        both = jnp.concatenate([grad_ref[:, block(k)], moment_ref[:, block(k)]], axis=1)
        twice = jnp.concatenate([both, both], axis=0)
        put_split(first_ref.at[k], dot(forth_ref[...], twice, NN))

    def over_columns(k):
        coeffs = dot(pair_ref[...], first_ref[k], NT)
        coeffs = coeffs[:128] + coeffs[128:]
        for h in range(2):
            hit = level == at_ref[h, row(k, groups), :]
            for n in range(2):
                part = coeffs[h * 64 : (h + 1) * 64, n * 128 : (n + 1) * 128]
                picked_ref[n, h, row(k, groups), :] = jnp.sum(
                    jnp.where(hit, part, 0.0), axis=0, keepdims=True
                )

    for step in (over_rows, over_columns):
        for k in range(groups):
            step(k)
    lane = lax.broadcasted_iota(jnp.int32, (groups, 128), 1)
    for n in range(2):
        front, back = picked_ref[n, 0, :groups], picked_ref[n, 1, :groups]
        front = front + pltpu.roll(front, 64, 1)
        back = back + pltpu.roll(back, 64, 1)
        out_ref[n] = jnp.where(lane < 64, front, back)


def scale_kernel(count, squares_ref, picked_ref, factor_ref, own_ref, send_ref):
    total = jnp.sum(jnp.sum(squares_ref[...], axis=0), axis=1, keepdims=True)
    mean_square = jnp.broadcast_to(total, (1, 128)) / count
    factor = jnp.minimum(1.0, clip_rms / jnp.sqrt(mean_square + 1e-06))
    factor_ref[...] = factor
    values = momentum_decay * picked_ref[1] + factor * picked_ref[0]
    listing = jnp.concatenate([values, picked_ref[2]], axis=0)
    own_ref[...] = listing
    send_ref[...] = jnp.broadcast_to(listing[None], send_ref.shape)


def unpack(listings, at_ref, value_ref):
    groups = listings[0].shape[0] // 2
    lane = lax.broadcasted_iota(jnp.int32, (groups, 128), 1)
    offsets = [listing[groups:] for listing in listings]
    for r in range(len(listings)):
        total = listings[r][:groups]
        for s in range(r):
            total = total + jnp.where(offsets[s] == offsets[r], listings[s][:groups], 0.0)
        values = duplicate(total)
        for h, offset in enumerate(duplicate(offsets[r])):
            value_ref[r, h, :groups] = values[h]
            at_ref[r, h, :groups] = jnp.where(lane < 64, offset, offset - 64.0)


def decode(at_ref, value_ref, sparse_ref, second_ref, back_ref, tall_ref, ready, emit):
    lists = at_ref.shape[0]
    groups = 2 * sparse_ref.shape[0]
    level = lax.broadcasted_iota(jnp.int32, (64, 128), 0).astype(jnp.float32)

    def scatter(t, carry):
        for k in range(2):
            for h in range(2):
                part = jnp.zeros((64, 128), jnp.float32)
                for r in range(lists):
                    hit = level == at_ref[r, h, row(2 * t + k, groups), :]
                    part = jnp.where(hit, value_ref[r, h, row(2 * t + k, groups), :], part)
                high, low = split(part)
                at = slice(k * 128 + h * 64, k * 128 + h * 64 + 64)
                sparse_ref[t, at, :128] = high
                sparse_ref[t, at, 128:] = low
        return carry

    lax.fori_loop(0, groups // 2, scatter, 0, unroll=3 if groups % 6 == 0 else 1)
    for copy in ready:
        copy.wait()
    for t in range(groups // 2):
        first = dot(back_ref[...], sparse_ref[t], NT)
        put_split(second_ref.at[t], first[:128] + first[128:])
    for t in range(groups // 2):
        decoded = dot(second_ref[t], tall_ref[...], NN)
        decoded = decoded[:, :128] + decoded[:, 128:]
        for k in range(2):
            emit(2 * t + k, decoded[k * 128 : (k + 1) * 128])


def fetch(sems, *pairs):
    copies = [pltpu.make_async_copy(source, target, sems.at[n]) for n, (source, target) in enumerate(pairs)]
    for copy in copies:
        copy.start()
    return copies


class Outlet:
    def __init__(self, source, target, sems, first_sem):
        self.source, self.target, self.sems, self.first_sem = source, target, sems, first_sem
        self.per = max(2, source.shape[1] // 128 // PARTS)
        self.copies = []

    def put(self, k, value):
        self.source[:, block(k)] = value.astype(self.source.dtype)
        if (k + 1) % self.per == 0:
            at = pl.ds((k + 1 - self.per) * 128, self.per * 128)
            copy = pltpu.make_async_copy(
                self.source.at[:, at],
                self.target.at[:, at],
                self.sems.at[self.first_sem + len(self.copies)],
            )
            copy.start()
            self.copies.append(copy)

    def wait(self):
        for copy in self.copies:
            copy.wait()


def own_kernel(
    own_ref, factor_ref, grad_ref, moment_ref, back_hbm, tall_hbm, new_moment_hbm,
    back_ref, tall_ref, at_ref, value_ref, sparse_ref, second_ref, out_ref, sems,
):
    ready = fetch(sems, (back_hbm, back_ref), (tall_hbm, tall_ref))
    factor = factor_ref[...]
    unpack([own_ref[...]], at_ref, value_ref)
    outlet = Outlet(out_ref, new_moment_hbm, sems, 2)

    def emit(k, decoded):
        blended = momentum_decay * moment_ref[:, block(k)].astype(jnp.float32)
        blended = blended + factor * grad_ref[:, block(k)].astype(jnp.float32)
        outlet.put(k, blended - decoded)

    decode(at_ref, value_ref, sparse_ref, second_ref, back_ref, tall_ref, ready, emit)
    outlet.wait()


def finish_kernel(
    all_ref, back_hbm, tall_hbm, weight_hbm, new_weight_hbm,
    back_ref, tall_ref, weight_ref, at_ref, value_ref, sparse_ref, second_ref, out_ref, sems,
):
    ready = fetch(sems, (back_hbm, back_ref), (tall_hbm, tall_ref), (weight_hbm, weight_ref))
    unpack([all_ref[r] for r in range(all_ref.shape[0])], at_ref, value_ref)
    outlet = Outlet(out_ref, new_weight_hbm, sems, 3)

    def emit(k, decoded):
        outlet.put(k, weight_ref[:, block(k)].astype(jnp.float32) - step_rate * decoded)

    decode(at_ref, value_ref, sparse_ref, second_ref, back_ref, tall_ref, ready, emit)
    outlet.wait()


def led_by(head, members):
    return [head] + [member for member in members if member != head]


def ring_groups(replicas, size):
    heads = (18, 22) if size == 32 else (0, 0)
    return [
        [r * size + member for member in led_by(heads[r % 2], range(size))] for r in range(replicas)
    ]


def chip_groups(replicas):
    chips = replicas // 2
    return [
        [(head - n) % chips * 2 + core for n in range(chips)] for core, head in enumerate((5, 6))
    ]


def body(grad, momentum, kept_index, weights):
    grad, momentum = grad[0], momentum[0]
    rows, cols = grad.shape
    ring = lax.axis_size("fsdp")
    replicas = lax.axis_size("rep")
    groups = cols // 128
    bf16, f32 = jnp.bfloat16, jnp.float32
    pair, back = tables()
    forth = jnp.asarray(np.concatenate(split_table(back.T), axis=1))
    back_wide = jnp.asarray(widen(back))
    pair_wide = jnp.asarray(widen(pair))
    pair_tall = jnp.asarray(np.ascontiguousarray(widen(pair.T).T))
    whole = pl.BlockSpec(memory_space=VMEM)
    hbm = pl.BlockSpec(memory_space=pl.ANY)
    params = pltpu.CompilerParams(vmem_limit_bytes=32 * 1024 * 1024)
    full = jax.ShapeDtypeStruct((rows, cols), bf16)
    square = jax.ShapeDtypeStruct((256, 256), bf16)

    squares, grad_near, moment_near, kept_near, forth_near, pair_near = pl.pallas_call(
        fetch_kernel,
        out_shape=(
            jax.ShapeDtypeStruct((ring, 1, 128), f32),
            full,
            full,
            jax.ShapeDtypeStruct(kept_index.shape[1:], jnp.int32),
            jax.ShapeDtypeStruct((128, 256), bf16),
            square,
        ),
        in_specs=[hbm] * 5,
        out_specs=(hbm,) + (whole,) * 5,
        scratch_shapes=[VMEM((ring, 1, 128), f32), pltpu.SemaphoreType.DMA((CHUNKS + 5,))],
        compiler_params=params,
        name="fetch",
    )(*in_hbm(grad, momentum, kept_index[0], forth, pair_wide))
    squares = lax.all_to_all(
        squares,
        ("rep", "fsdp"),
        0,
        0,
        tiled=True,
        axis_index_groups=ring_groups(replicas, ring),
    )

    picked = pl.pallas_call(
        pick_kernel,
        out_shape=jax.ShapeDtypeStruct((3, groups, 128), f32),
        in_specs=[whole] * 5,
        out_specs=whole,
        scratch_shapes=[
            VMEM((2, groups // 2 + SPARE, 128), jnp.int32),
            VMEM((2, groups + SPARE, 128), f32),
            VMEM((groups + SPARE, 128), f32),
            VMEM((groups, 256, 256), bf16),
            VMEM((2, 2, groups + SPARE, 128), f32),
        ],
        compiler_params=params,
        cost_estimate=pl.CostEstimate(
            flops=2 * 2 * 10 * 128 * 128 * cols, bytes_accessed=4 * rows * cols, transcendentals=0
        ),
        name="pick",
    )(kept_near, grad_near, moment_near, forth_near, pair_near)

    factor, own, send = pl.pallas_call(
        functools.partial(scale_kernel, float(rows * ring * cols)),
        out_shape=(
            jax.ShapeDtypeStruct((1, 128), f32),
            jax.ShapeDtypeStruct((2 * groups, 128), f32),
            jax.ShapeDtypeStruct((replicas // 2, 2 * groups, 128), f32),
        ),
        in_specs=[whole] * 2,
        out_specs=(whole,) * 3,
        compiler_params=params,
        name="scale",
    )(squares, picked)

    every = lax.all_to_all(
        send, "rep", 0, 0, tiled=True, axis_index_groups=chip_groups(replicas)
    )
    cores = [[chip * 2 + core for core in range(2)] for chip in range(replicas // 2)]
    every = lax.all_gather(every, "rep", axis=0, tiled=True, axis_index_groups=cores)

    def work(lists):
        return [
            VMEM((lists, 2, groups + SPARE, 128), f32),
            VMEM((lists, 2, groups + SPARE, 128), f32),
            VMEM((groups // 2, 256, 256), bf16),
            VMEM((groups // 2, 256, 256), bf16),
            VMEM((rows, cols), bf16),
            pltpu.SemaphoreType.DMA((3 + groups // 2,)),
        ]

    new_momentum = pl.pallas_call(
        own_kernel,
        out_shape=full,
        in_specs=[whole] * 4 + [hbm] * 2,
        out_specs=hbm,
        scratch_shapes=[VMEM((256, 256), bf16)] * 2 + work(1),
        compiler_params=params,
        cost_estimate=pl.CostEstimate(
            flops=2 * 2 * 10 * 128 * 128 * cols, bytes_accessed=4 * rows * cols, transcendentals=0
        ),
        name="own",
    )(own, factor, grad_near, moment_near, *in_hbm(back_wide, pair_tall))

    new_weights = pl.pallas_call(
        finish_kernel,
        out_shape=full,
        in_specs=[whole] + [hbm] * 3,
        out_specs=hbm,
        scratch_shapes=[VMEM((256, 256), bf16)] * 2 + [VMEM((rows, cols), bf16)] + work(replicas),
        compiler_params=params,
        name="finish",
    )(every, *in_hbm(back_wide, pair_tall, weights))
    return (new_momentum[None], new_weights)


def solution(mesh):
    in_specs = (
        P("rep", "fsdp", None),
        P("rep", "fsdp", None),
        P("rep", "fsdp", None),
        P("fsdp", None),
    )
    out_specs = (P("rep", "fsdp", None), P("fsdp", None))
    return jax.shard_map(body, mesh=mesh, in_specs=in_specs, out_specs=out_specs, check_vma=False)
```

```python
import functools

import jax
import jax.numpy as jnp
import ml_dtypes
import numpy as np
from jax import lax
from jax.experimental import pallas as pl
from jax.experimental.pallas import tpu as pltpu
from jax.sharding import PartitionSpec as P

clip_rms = 0.5
momentum_decay = 0.9
step_rate = 0.5
VMEM = pltpu.VMEM
SPARE = 8
PARTS = 6
CHUNKS = 2
NN = (((1,), (0,)), ((), ()))
NT = (((1,), (1,)), ((), ()))


def split_table(table):
    high = table.astype(ml_dtypes.bfloat16)
    low = (table - high.astype(np.float64)).astype(ml_dtypes.bfloat16)
    return high, low


def tables():
    u = np.arange(64, dtype=np.float64)[:, None]
    x = np.arange(64, dtype=np.float64)[None, :]
    weight = np.where(u == 0, np.sqrt(1.0 / 64.0), np.sqrt(2.0 / 64.0))
    dct = weight * np.cos(np.pi * (2.0 * x + 1.0) * u / 128.0)
    pair = np.kron(np.eye(2), dct)
    rows = np.zeros((2, 64, 2, 2, 32))
    by_parity = dct.reshape(32, 2, 64)
    for i in range(2):
        rows[i, :, :, i, :] = by_parity.transpose(2, 1, 0)
    return pair, rows.reshape(128, 128)


def widen(table):
    high, low = split_table(table)
    return np.block([[high, high], [low, low]])


def split(value):
    high = value.astype(jnp.bfloat16)
    low = (value - high.astype(jnp.float32)).astype(jnp.bfloat16)
    return high, low


def dot(left, right, dims):
    return lax.dot_general(left, right, dims, preferred_element_type=jnp.float32)


def duplicate(packed):
    lane = lax.broadcasted_iota(jnp.int32, packed.shape, 1)
    other = pltpu.roll(packed, 64, 1)
    return jnp.where(lane < 64, packed, other), jnp.where(lane < 64, other, packed)


def block(k):
    return pl.ds(k * 128 if isinstance(k, int) else pl.multiple_of(k * 128, 128), 128)


def row(k, groups):
    return pl.ds((k % 2) * (groups // 2) + k // 2, 1)


def in_hbm(*arrays):
    return [pltpu.with_memory_space_constraint(array, pltpu.HBM) for array in arrays]


def put_split(ref, value):
    high, low = split(value)
    for n in range(value.shape[1] // 128):
        ref[n * 128 : (n + 1) * 128, :128] = high[:, n * 128 : (n + 1) * 128]
        ref[n * 128 : (n + 1) * 128, 128:] = low[:, n * 128 : (n + 1) * 128]


def fetch_kernel(grad_hbm, *refs):
    count = (len(refs) - 4) // 2
    sources, out_hbm, grad_ref = refs[:count], refs[count], refs[count + 1]
    targets, out_ref, sems = refs[count + 2 : -2], refs[-2], refs[-1]
    width = grad_ref.shape[1] // CHUNKS
    copies = [
        pltpu.make_async_copy(
            grad_hbm.at[:, pl.ds(n * width, width)],
            grad_ref.at[:, pl.ds(n * width, width)],
            sems.at[n],
        )
        for n in range(CHUNKS)
    ]
    copies += [
        pltpu.make_async_copy(source, target, sems.at[CHUNKS + n])
        for n, (source, target) in enumerate(zip(sources, targets))
    ]
    for copy in copies:
        copy.start()
    total = jnp.zeros((8, 128), jnp.float32)
    for n in range(CHUNKS):
        copies[n].wait()
        for k in range(n * width // 128, (n + 1) * width // 128):
            value = grad_ref[:, block(k)].astype(jnp.float32)
            total = total + jnp.sum((value * value).reshape(-1, 8, 128), axis=0)
    out_ref[...] = jnp.broadcast_to(
        jnp.sum(total, axis=0, keepdims=True)[None], out_ref.shape
    )
    copies.append(pltpu.make_async_copy(out_ref, out_hbm, sems.at[len(copies)]))
    copies[-1].start()
    for copy in copies[CHUNKS:]:
        copy.wait()


def pick_kernel(
    kept_ref, grad_ref, moment_ref, forth_ref, pair_ref, out_ref, listed_ref, at_ref, placed_ref, first_ref, picked_ref
):
    groups = out_ref.shape[1]
    half = groups // 2
    lane = lax.broadcasted_iota(jnp.int32, (half, 128), 1)
    kept = kept_ref[...]
    for i in range(2):
        for n in range(half):
            listed_ref[i, n : n + 1] = kept[i : i + 1, n * 128 : (n + 1) * 128]
    offsets = [(listed_ref[i, :half] & 127).astype(jnp.float32) for i in range(2)]
    for q in range(2):
        placed = []
        for h in range(2):
            here = (2 * q + h) * 32
            front = pltpu.roll(offsets[0], (128 - here) % 128, 1)
            back = pltpu.roll(offsets[1], (160 - here) % 128, 1)
            placed.append(jnp.where(lane < 32, front, back))
            there = pltpu.roll(placed[h], 64, 1)
            at_ref[h, q * half : (q + 1) * half] = jnp.where(lane < 64, placed[h], there - 64.0)
        placed_ref[q * half : (q + 1) * half] = jnp.where(
            lane < 64, placed[0], pltpu.roll(placed[1], 64, 1)
        )
    out_ref[2] = placed_ref[:groups]
    level = lax.broadcasted_iota(jnp.int32, (64, 128), 0).astype(jnp.float32)

    def over_rows(k):
        both = jnp.concatenate([grad_ref[:, block(k)], moment_ref[:, block(k)]], axis=1)
        twice = jnp.concatenate([both, both], axis=0)
        put_split(first_ref.at[k], dot(forth_ref[...], twice, NN))

    def over_columns(k):
        coeffs = dot(pair_ref[...], first_ref[k], NT)
        coeffs = coeffs[:128] + coeffs[128:]
        for h in range(2):
            hit = level == at_ref[h, row(k, groups), :]
            for n in range(2):
                part = coeffs[h * 64 : (h + 1) * 64, n * 128 : (n + 1) * 128]
                picked_ref[n, h, row(k, groups), :] = jnp.sum(
                    jnp.where(hit, part, 0.0), axis=0, keepdims=True
                )

    for step in (over_rows, over_columns):
        for k in range(groups):
            step(k)
    lane = lax.broadcasted_iota(jnp.int32, (groups, 128), 1)
    for n in range(2):
        front, back = picked_ref[n, 0, :groups], picked_ref[n, 1, :groups]
        front = front + pltpu.roll(front, 64, 1)
        back = back + pltpu.roll(back, 64, 1)
        out_ref[n] = jnp.where(lane < 64, front, back)


def scale_kernel(count, squares_ref, picked_ref, factor_ref, own_ref, send_ref):
    total = jnp.sum(jnp.sum(squares_ref[...], axis=0), axis=1, keepdims=True)
    mean_square = jnp.broadcast_to(total, (1, 128)) / count
    factor = jnp.minimum(1.0, clip_rms / jnp.sqrt(mean_square + 1e-06))
    factor_ref[...] = factor
    values = momentum_decay * picked_ref[1] + factor * picked_ref[0]
    listing = jnp.concatenate([values, picked_ref[2]], axis=0)
    own_ref[...] = listing
    send_ref[...] = jnp.broadcast_to(listing[None], send_ref.shape)


def unpack(listings, at_ref, value_ref):
    groups = listings[0].shape[0] // 2
    lane = lax.broadcasted_iota(jnp.int32, (groups, 128), 1)
    offsets = [listing[groups:] for listing in listings]
    for r in range(len(listings)):
        total = listings[r][:groups]
        for s in range(r):
            total = total + jnp.where(offsets[s] == offsets[r], listings[s][:groups], 0.0)
        values = duplicate(total)
        for h, offset in enumerate(duplicate(offsets[r])):
            value_ref[r, h, :groups] = values[h]
            at_ref[r, h, :groups] = jnp.where(lane < 64, offset, offset - 64.0)


def decode(at_ref, value_ref, sparse_ref, second_ref, back_ref, tall_ref, ready, emit):
    lists = at_ref.shape[0]
    groups = 2 * sparse_ref.shape[0]
    level = lax.broadcasted_iota(jnp.int32, (64, 128), 0).astype(jnp.float32)

    def scatter(t, carry):
        for k in range(2):
            for h in range(2):
                part = jnp.zeros((64, 128), jnp.float32)
                for r in range(lists):
                    hit = level == at_ref[r, h, row(2 * t + k, groups), :]
                    part = jnp.where(hit, value_ref[r, h, row(2 * t + k, groups), :], part)
                high, low = split(part)
                at = slice(k * 128 + h * 64, k * 128 + h * 64 + 64)
                sparse_ref[t, at, :128] = high
                sparse_ref[t, at, 128:] = low
        return carry

    lax.fori_loop(0, groups // 2, scatter, 0, unroll=3 if groups % 6 == 0 else 1)
    for copy in ready:
        copy.wait()
    for t in range(groups // 2):
        first = dot(back_ref[...], sparse_ref[t], NT)
        put_split(second_ref.at[t], first[:128] + first[128:])
    for t in range(groups // 2):
        decoded = dot(second_ref[t], tall_ref[...], NN)
        decoded = decoded[:, :128] + decoded[:, 128:]
        for k in range(2):
            emit(2 * t + k, decoded[k * 128 : (k + 1) * 128])


def fetch(sems, *pairs):
    copies = [pltpu.make_async_copy(source, target, sems.at[n]) for n, (source, target) in enumerate(pairs)]
    for copy in copies:
        copy.start()
    return copies


class Outlet:
    def __init__(self, source, target, sems, first_sem):
        self.source, self.target, self.sems, self.first_sem = source, target, sems, first_sem
        self.per = max(2, source.shape[1] // 128 // PARTS)
        self.copies = []

    def put(self, k, value):
        self.source[:, block(k)] = value.astype(self.source.dtype)
        if (k + 1) % self.per == 0:
            at = pl.ds((k + 1 - self.per) * 128, self.per * 128)
            copy = pltpu.make_async_copy(
                self.source.at[:, at],
                self.target.at[:, at],
                self.sems.at[self.first_sem + len(self.copies)],
            )
            copy.start()
            self.copies.append(copy)

    def wait(self):
        for copy in self.copies:
            copy.wait()


def own_kernel(
    own_ref, factor_ref, grad_ref, moment_ref, back_hbm, tall_hbm, new_moment_hbm,
    back_ref, tall_ref, at_ref, value_ref, sparse_ref, second_ref, out_ref, sems,
):
    ready = fetch(sems, (back_hbm, back_ref), (tall_hbm, tall_ref))
    factor = factor_ref[...]
    unpack([own_ref[...]], at_ref, value_ref)
    outlet = Outlet(out_ref, new_moment_hbm, sems, 2)

    def emit(k, decoded):
        blended = momentum_decay * moment_ref[:, block(k)].astype(jnp.float32)
        blended = blended + factor * grad_ref[:, block(k)].astype(jnp.float32)
        outlet.put(k, blended - decoded)

    decode(at_ref, value_ref, sparse_ref, second_ref, back_ref, tall_ref, ready, emit)
    outlet.wait()


def finish_kernel(
    all_ref, back_hbm, tall_hbm, weight_hbm, new_weight_hbm,
    back_ref, tall_ref, weight_ref, at_ref, value_ref, sparse_ref, second_ref, out_ref, sems,
):
    ready = fetch(sems, (back_hbm, back_ref), (tall_hbm, tall_ref), (weight_hbm, weight_ref))
    unpack([all_ref[r] for r in range(all_ref.shape[0])], at_ref, value_ref)
    outlet = Outlet(out_ref, new_weight_hbm, sems, 3)

    def emit(k, decoded):
        outlet.put(k, weight_ref[:, block(k)].astype(jnp.float32) - step_rate * decoded)

    decode(at_ref, value_ref, sparse_ref, second_ref, back_ref, tall_ref, ready, emit)
    outlet.wait()


def led_by(head, members):
    return [head] + [member for member in members if member != head]


def ring_groups(replicas, size):
    heads = (18, 22) if size == 32 else (0, 0)
    return [
        [r * size + member for member in led_by(heads[r % 2], range(size))] for r in range(replicas)
    ]


def chip_groups(replicas):
    chips = replicas // 2
    return [
        [(head - n) % chips * 2 + core for n in range(chips)] for core, head in enumerate((4, 6))
    ]


def body(grad, momentum, kept_index, weights):
    grad, momentum = grad[0], momentum[0]
    rows, cols = grad.shape
    ring = lax.axis_size("fsdp")
    replicas = lax.axis_size("rep")
    groups = cols // 128
    bf16, f32 = jnp.bfloat16, jnp.float32
    pair, back = tables()
    forth = jnp.asarray(np.concatenate(split_table(back.T), axis=1))
    back_wide = jnp.asarray(widen(back))
    pair_wide = jnp.asarray(widen(pair))
    pair_tall = jnp.asarray(np.ascontiguousarray(widen(pair.T).T))
    whole = pl.BlockSpec(memory_space=VMEM)
    hbm = pl.BlockSpec(memory_space=pl.ANY)
    params = pltpu.CompilerParams(vmem_limit_bytes=32 * 1024 * 1024)
    full = jax.ShapeDtypeStruct((rows, cols), bf16)
    square = jax.ShapeDtypeStruct((256, 256), bf16)

    squares, grad_near, moment_near, kept_near, forth_near, pair_near = pl.pallas_call(
        fetch_kernel,
        out_shape=(
            jax.ShapeDtypeStruct((ring, 1, 128), f32),
            full,
            full,
            jax.ShapeDtypeStruct(kept_index.shape[1:], jnp.int32),
            jax.ShapeDtypeStruct((128, 256), bf16),
            square,
        ),
        in_specs=[hbm] * 5,
        out_specs=(hbm,) + (whole,) * 5,
        scratch_shapes=[VMEM((ring, 1, 128), f32), pltpu.SemaphoreType.DMA((CHUNKS + 5,))],
        compiler_params=params,
        name="fetch",
    )(*in_hbm(grad, momentum, kept_index[0], forth, pair_wide))
    squares = lax.all_to_all(
        squares,
        ("rep", "fsdp"),
        0,
        0,
        tiled=True,
        axis_index_groups=ring_groups(replicas, ring),
    )

    picked = pl.pallas_call(
        pick_kernel,
        out_shape=jax.ShapeDtypeStruct((3, groups, 128), f32),
        in_specs=[whole] * 5,
        out_specs=whole,
        scratch_shapes=[
            VMEM((2, groups // 2 + SPARE, 128), jnp.int32),
            VMEM((2, groups + SPARE, 128), f32),
            VMEM((groups + SPARE, 128), f32),
            VMEM((groups, 256, 256), bf16),
            VMEM((2, 2, groups + SPARE, 128), f32),
        ],
        compiler_params=params,
        cost_estimate=pl.CostEstimate(
            flops=2 * 2 * 10 * 128 * 128 * cols, bytes_accessed=4 * rows * cols, transcendentals=0
        ),
        name="pick",
    )(kept_near, grad_near, moment_near, forth_near, pair_near)

    factor, own, send = pl.pallas_call(
        functools.partial(scale_kernel, float(rows * ring * cols)),
        out_shape=(
            jax.ShapeDtypeStruct((1, 128), f32),
            jax.ShapeDtypeStruct((2 * groups, 128), f32),
            jax.ShapeDtypeStruct((replicas // 2, 2 * groups, 128), f32),
        ),
        in_specs=[whole] * 2,
        out_specs=(whole,) * 3,
        compiler_params=params,
        name="scale",
    )(squares, picked)

    every = lax.all_to_all(
        send, "rep", 0, 0, tiled=True, axis_index_groups=chip_groups(replicas)
    )
    cores = [[chip * 2 + core for core in range(2)] for chip in range(replicas // 2)]
    every = lax.all_gather(every, "rep", axis=0, tiled=True, axis_index_groups=cores)

    def work(lists):
        return [
            VMEM((lists, 2, groups + SPARE, 128), f32),
            VMEM((lists, 2, groups + SPARE, 128), f32),
            VMEM((groups // 2, 256, 256), bf16),
            VMEM((groups // 2, 256, 256), bf16),
            VMEM((rows, cols), bf16),
            pltpu.SemaphoreType.DMA((3 + groups // 2,)),
        ]

    new_momentum = pl.pallas_call(
        own_kernel,
        out_shape=full,
        in_specs=[whole] * 4 + [hbm] * 2,
        out_specs=hbm,
        scratch_shapes=[VMEM((256, 256), bf16)] * 2 + work(1),
        compiler_params=params,
        cost_estimate=pl.CostEstimate(
            flops=2 * 2 * 10 * 128 * 128 * cols, bytes_accessed=4 * rows * cols, transcendentals=0
        ),
        name="own",
    )(own, factor, grad_near, moment_near, *in_hbm(back_wide, pair_tall))

    new_weights = pl.pallas_call(
        finish_kernel,
        out_shape=full,
        in_specs=[whole] + [hbm] * 3,
        out_specs=hbm,
        scratch_shapes=[VMEM((256, 256), bf16)] * 2 + [VMEM((rows, cols), bf16)] + work(replicas),
        compiler_params=params,
        name="finish",
    )(every, *in_hbm(back_wide, pair_tall, weights))
    return (new_momentum[None], new_weights)


def solution(mesh):
    in_specs = (
        P("rep", "fsdp", None),
        P("rep", "fsdp", None),
        P("rep", "fsdp", None),
        P("fsdp", None),
    )
    out_specs = (P("rep", "fsdp", None), P("fsdp", None))
    return jax.shard_map(body, mesh=mesh, in_specs=in_specs, out_specs=out_specs, check_vma=False)
```

```python
import functools

import jax
import jax.numpy as jnp
import ml_dtypes
import numpy as np
from jax import lax
from jax.experimental import pallas as pl
from jax.experimental.pallas import tpu as pltpu
from jax.sharding import PartitionSpec as P

clip_rms = 0.5
momentum_decay = 0.9
step_rate = 0.5
VMEM = pltpu.VMEM
SPARE = 8
PARTS = 6
CHUNKS = 2
NN = (((1,), (0,)), ((), ()))
NT = (((1,), (1,)), ((), ()))


def split_table(table):
    high = table.astype(ml_dtypes.bfloat16)
    low = (table - high.astype(np.float64)).astype(ml_dtypes.bfloat16)
    return high, low


def tables():
    u = np.arange(64, dtype=np.float64)[:, None]
    x = np.arange(64, dtype=np.float64)[None, :]
    weight = np.where(u == 0, np.sqrt(1.0 / 64.0), np.sqrt(2.0 / 64.0))
    dct = weight * np.cos(np.pi * (2.0 * x + 1.0) * u / 128.0)
    pair = np.kron(np.eye(2), dct)
    rows = np.zeros((2, 64, 2, 2, 32))
    by_parity = dct.reshape(32, 2, 64)
    for i in range(2):
        rows[i, :, :, i, :] = by_parity.transpose(2, 1, 0)
    return pair, rows.reshape(128, 128)


def widen(table):
    high, low = split_table(table)
    return np.block([[high, high], [low, low]])


def split(value):
    high = value.astype(jnp.bfloat16)
    low = (value - high.astype(jnp.float32)).astype(jnp.bfloat16)
    return high, low


def dot(left, right, dims):
    return lax.dot_general(left, right, dims, preferred_element_type=jnp.float32)


def duplicate(packed):
    lane = lax.broadcasted_iota(jnp.int32, packed.shape, 1)
    other = pltpu.roll(packed, 64, 1)
    return jnp.where(lane < 64, packed, other), jnp.where(lane < 64, other, packed)


def block(k):
    return pl.ds(k * 128 if isinstance(k, int) else pl.multiple_of(k * 128, 128), 128)


def row(k, groups):
    return pl.ds((k % 2) * (groups // 2) + k // 2, 1)


def in_hbm(*arrays):
    return [pltpu.with_memory_space_constraint(array, pltpu.HBM) for array in arrays]


def put_split(ref, value):
    high, low = split(value)
    for n in range(value.shape[1] // 128):
        ref[n * 128 : (n + 1) * 128, :128] = high[:, n * 128 : (n + 1) * 128]
        ref[n * 128 : (n + 1) * 128, 128:] = low[:, n * 128 : (n + 1) * 128]


def fetch_kernel(grad_hbm, *refs):
    count = (len(refs) - 4) // 2
    sources, out_hbm, grad_ref = refs[:count], refs[count], refs[count + 1]
    targets, out_ref, sems = refs[count + 2 : -2], refs[-2], refs[-1]
    width = grad_ref.shape[1] // CHUNKS
    copies = [
        pltpu.make_async_copy(
            grad_hbm.at[:, pl.ds(n * width, width)],
            grad_ref.at[:, pl.ds(n * width, width)],
            sems.at[n],
        )
        for n in range(CHUNKS)
    ]
    copies += [
        pltpu.make_async_copy(source, target, sems.at[CHUNKS + n])
        for n, (source, target) in enumerate(zip(sources, targets))
    ]
    for copy in copies:
        copy.start()
    total = jnp.zeros((8, 128), jnp.float32)
    for n in range(CHUNKS):
        copies[n].wait()
        for k in range(n * width // 128, (n + 1) * width // 128):
            value = grad_ref[:, block(k)].astype(jnp.float32)
            total = total + jnp.sum((value * value).reshape(-1, 8, 128), axis=0)
    out_ref[...] = jnp.broadcast_to(
        jnp.sum(total, axis=0, keepdims=True)[None], out_ref.shape
    )
    copies.append(pltpu.make_async_copy(out_ref, out_hbm, sems.at[len(copies)]))
    copies[-1].start()
    for copy in copies[CHUNKS:]:
        copy.wait()


def pick_kernel(
    kept_ref, grad_ref, moment_ref, forth_ref, pair_ref, out_ref, listed_ref, at_ref, placed_ref, first_ref, picked_ref
):
    groups = out_ref.shape[1]
    half = groups // 2
    lane = lax.broadcasted_iota(jnp.int32, (half, 128), 1)
    kept = kept_ref[...]
    for i in range(2):
        for n in range(half):
            listed_ref[i, n : n + 1] = kept[i : i + 1, n * 128 : (n + 1) * 128]
    offsets = [(listed_ref[i, :half] & 127).astype(jnp.float32) for i in range(2)]
    for q in range(2):
        placed = []
        for h in range(2):
            here = (2 * q + h) * 32
            front = pltpu.roll(offsets[0], (128 - here) % 128, 1)
            back = pltpu.roll(offsets[1], (160 - here) % 128, 1)
            placed.append(jnp.where(lane < 32, front, back))
            there = pltpu.roll(placed[h], 64, 1)
            at_ref[h, q * half : (q + 1) * half] = jnp.where(lane < 64, placed[h], there - 64.0)
        placed_ref[q * half : (q + 1) * half] = jnp.where(
            lane < 64, placed[0], pltpu.roll(placed[1], 64, 1)
        )
    out_ref[2] = placed_ref[:groups]
    level = lax.broadcasted_iota(jnp.int32, (64, 128), 0).astype(jnp.float32)

    def over_rows(k):
        both = jnp.concatenate([grad_ref[:, block(k)], moment_ref[:, block(k)]], axis=1)
        twice = jnp.concatenate([both, both], axis=0)
        put_split(first_ref.at[k], dot(forth_ref[...], twice, NN))

    def over_columns(k):
        coeffs = dot(pair_ref[...], first_ref[k], NT)
        coeffs = coeffs[:128] + coeffs[128:]
        for h in range(2):
            hit = level == at_ref[h, row(k, groups), :]
            for n in range(2):
                part = coeffs[h * 64 : (h + 1) * 64, n * 128 : (n + 1) * 128]
                picked_ref[n, h, row(k, groups), :] = jnp.sum(
                    jnp.where(hit, part, 0.0), axis=0, keepdims=True
                )

    for step in (over_rows, over_columns):
        for k in range(groups):
            step(k)
    lane = lax.broadcasted_iota(jnp.int32, (groups, 128), 1)
    for n in range(2):
        front, back = picked_ref[n, 0, :groups], picked_ref[n, 1, :groups]
        front = front + pltpu.roll(front, 64, 1)
        back = back + pltpu.roll(back, 64, 1)
        out_ref[n] = jnp.where(lane < 64, front, back)


def scale_kernel(count, squares_ref, picked_ref, factor_ref, own_ref, send_ref):
    total = jnp.sum(jnp.sum(squares_ref[...], axis=0), axis=1, keepdims=True)
    mean_square = jnp.broadcast_to(total, (1, 128)) / count
    factor = jnp.minimum(1.0, clip_rms / jnp.sqrt(mean_square + 1e-06))
    factor_ref[...] = factor
    values = momentum_decay * picked_ref[1] + factor * picked_ref[0]
    listing = jnp.concatenate([values, picked_ref[2]], axis=0)
    own_ref[...] = listing
    send_ref[...] = jnp.broadcast_to(listing[None], send_ref.shape)


def unpack(listings, at_ref, value_ref):
    groups = listings[0].shape[0] // 2
    lane = lax.broadcasted_iota(jnp.int32, (groups, 128), 1)
    offsets = [listing[groups:] for listing in listings]
    for r in range(len(listings)):
        total = listings[r][:groups]
        for s in range(r):
            total = total + jnp.where(offsets[s] == offsets[r], listings[s][:groups], 0.0)
        values = duplicate(total)
        for h, offset in enumerate(duplicate(offsets[r])):
            value_ref[r, h, :groups] = values[h]
            at_ref[r, h, :groups] = jnp.where(lane < 64, offset, offset - 64.0)


def decode(at_ref, value_ref, sparse_ref, second_ref, back_ref, tall_ref, ready, emit):
    lists = at_ref.shape[0]
    groups = 2 * sparse_ref.shape[0]
    level = lax.broadcasted_iota(jnp.int32, (64, 128), 0).astype(jnp.float32)

    def scatter(t, carry):
        for k in range(2):
            for h in range(2):
                part = jnp.zeros((64, 128), jnp.float32)
                for r in range(lists):
                    hit = level == at_ref[r, h, row(2 * t + k, groups), :]
                    part = jnp.where(hit, value_ref[r, h, row(2 * t + k, groups), :], part)
                high, low = split(part)
                at = slice(k * 128 + h * 64, k * 128 + h * 64 + 64)
                sparse_ref[t, at, :128] = high
                sparse_ref[t, at, 128:] = low
        return carry

    lax.fori_loop(0, groups // 2, scatter, 0, unroll=4 if groups % 8 == 0 else 1)
    for copy in ready:
        copy.wait()
    for t in range(groups // 2):
        first = dot(back_ref[...], sparse_ref[t], NT)
        put_split(second_ref.at[t], first[:128] + first[128:])
    for t in range(groups // 2):
        decoded = dot(second_ref[t], tall_ref[...], NN)
        decoded = decoded[:, :128] + decoded[:, 128:]
        for k in range(2):
            emit(2 * t + k, decoded[k * 128 : (k + 1) * 128])


def fetch(sems, *pairs):
    copies = [pltpu.make_async_copy(source, target, sems.at[n]) for n, (source, target) in enumerate(pairs)]
    for copy in copies:
        copy.start()
    return copies


class Outlet:
    def __init__(self, source, target, sems, first_sem):
        self.source, self.target, self.sems, self.first_sem = source, target, sems, first_sem
        self.per = max(2, source.shape[1] // 128 // PARTS)
        self.copies = []

    def put(self, k, value):
        self.source[:, block(k)] = value.astype(self.source.dtype)
        if (k + 1) % self.per == 0:
            at = pl.ds((k + 1 - self.per) * 128, self.per * 128)
            copy = pltpu.make_async_copy(
                self.source.at[:, at],
                self.target.at[:, at],
                self.sems.at[self.first_sem + len(self.copies)],
            )
            copy.start()
            self.copies.append(copy)

    def wait(self):
        for copy in self.copies:
            copy.wait()


def own_kernel(
    own_ref, factor_ref, grad_ref, moment_ref, back_hbm, tall_hbm, new_moment_hbm,
    back_ref, tall_ref, at_ref, value_ref, sparse_ref, second_ref, out_ref, sems,
):
    ready = fetch(sems, (back_hbm, back_ref), (tall_hbm, tall_ref))
    factor = factor_ref[...]
    unpack([own_ref[...]], at_ref, value_ref)
    outlet = Outlet(out_ref, new_moment_hbm, sems, 2)

    def emit(k, decoded):
        blended = momentum_decay * moment_ref[:, block(k)].astype(jnp.float32)
        blended = blended + factor * grad_ref[:, block(k)].astype(jnp.float32)
        outlet.put(k, blended - decoded)

    decode(at_ref, value_ref, sparse_ref, second_ref, back_ref, tall_ref, ready, emit)
    outlet.wait()


def finish_kernel(
    all_ref, back_hbm, tall_hbm, weight_hbm, new_weight_hbm,
    back_ref, tall_ref, weight_ref, at_ref, value_ref, sparse_ref, second_ref, out_ref, sems,
):
    ready = fetch(sems, (back_hbm, back_ref), (tall_hbm, tall_ref), (weight_hbm, weight_ref))
    unpack([all_ref[r] for r in range(all_ref.shape[0])], at_ref, value_ref)
    outlet = Outlet(out_ref, new_weight_hbm, sems, 3)

    def emit(k, decoded):
        outlet.put(k, weight_ref[:, block(k)].astype(jnp.float32) - step_rate * decoded)

    decode(at_ref, value_ref, sparse_ref, second_ref, back_ref, tall_ref, ready, emit)
    outlet.wait()


def led_by(head, members):
    return [head] + [member for member in members if member != head]


def ring_groups(replicas, size):
    heads = (18, 22) if size == 32 else (0, 0)
    return [
        [r * size + member for member in led_by(heads[r % 2], range(size))] for r in range(replicas)
    ]


def chip_groups(replicas):
    chips = replicas // 2
    return [
        [(head - n) % chips * 2 + core for n in range(chips)] for core, head in enumerate((5, 6))
    ]


def body(grad, momentum, kept_index, weights):
    grad, momentum = grad[0], momentum[0]
    rows, cols = grad.shape
    ring = lax.axis_size("fsdp")
    replicas = lax.axis_size("rep")
    groups = cols // 128
    bf16, f32 = jnp.bfloat16, jnp.float32
    pair, back = tables()
    forth = jnp.asarray(np.concatenate(split_table(back.T), axis=1))
    back_wide = jnp.asarray(widen(back))
    pair_wide = jnp.asarray(widen(pair))
    pair_tall = jnp.asarray(np.ascontiguousarray(widen(pair.T).T))
    whole = pl.BlockSpec(memory_space=VMEM)
    hbm = pl.BlockSpec(memory_space=pl.ANY)
    params = pltpu.CompilerParams(vmem_limit_bytes=32 * 1024 * 1024)
    full = jax.ShapeDtypeStruct((rows, cols), bf16)
    square = jax.ShapeDtypeStruct((256, 256), bf16)

    squares, grad_near, moment_near, kept_near, forth_near, pair_near = pl.pallas_call(
        fetch_kernel,
        out_shape=(
            jax.ShapeDtypeStruct((ring, 1, 128), f32),
            full,
            full,
            jax.ShapeDtypeStruct(kept_index.shape[1:], jnp.int32),
            jax.ShapeDtypeStruct((128, 256), bf16),
            square,
        ),
        in_specs=[hbm] * 5,
        out_specs=(hbm,) + (whole,) * 5,
        scratch_shapes=[VMEM((ring, 1, 128), f32), pltpu.SemaphoreType.DMA((CHUNKS + 5,))],
        compiler_params=params,
        name="fetch",
    )(*in_hbm(grad, momentum, kept_index[0], forth, pair_wide))
    squares = lax.all_to_all(
        squares,
        ("rep", "fsdp"),
        0,
        0,
        tiled=True,
        axis_index_groups=ring_groups(replicas, ring),
    )

    picked = pl.pallas_call(
        pick_kernel,
        out_shape=jax.ShapeDtypeStruct((3, groups, 128), f32),
        in_specs=[whole] * 5,
        out_specs=whole,
        scratch_shapes=[
            VMEM((2, groups // 2 + SPARE, 128), jnp.int32),
            VMEM((2, groups + SPARE, 128), f32),
            VMEM((groups + SPARE, 128), f32),
            VMEM((groups, 256, 256), bf16),
            VMEM((2, 2, groups + SPARE, 128), f32),
        ],
        compiler_params=params,
        cost_estimate=pl.CostEstimate(
            flops=2 * 2 * 10 * 128 * 128 * cols, bytes_accessed=4 * rows * cols, transcendentals=0
        ),
        name="pick",
    )(kept_near, grad_near, moment_near, forth_near, pair_near)

    factor, own, send = pl.pallas_call(
        functools.partial(scale_kernel, float(rows * ring * cols)),
        out_shape=(
            jax.ShapeDtypeStruct((1, 128), f32),
            jax.ShapeDtypeStruct((2 * groups, 128), f32),
            jax.ShapeDtypeStruct((replicas // 2, 2 * groups, 128), f32),
        ),
        in_specs=[whole] * 2,
        out_specs=(whole,) * 3,
        compiler_params=params,
        name="scale",
    )(squares, picked)

    every = lax.all_to_all(
        send, "rep", 0, 0, tiled=True, axis_index_groups=chip_groups(replicas)
    )
    cores = [[chip * 2 + core for core in range(2)] for chip in range(replicas // 2)]
    every = lax.all_gather(every, "rep", axis=0, tiled=True, axis_index_groups=cores)

    def work(lists):
        return [
            VMEM((lists, 2, groups + SPARE, 128), f32),
            VMEM((lists, 2, groups + SPARE, 128), f32),
            VMEM((groups // 2, 256, 256), bf16),
            VMEM((groups // 2, 256, 256), bf16),
            VMEM((rows, cols), bf16),
            pltpu.SemaphoreType.DMA((3 + groups // 2,)),
        ]

    new_momentum = pl.pallas_call(
        own_kernel,
        out_shape=full,
        in_specs=[whole] * 4 + [hbm] * 2,
        out_specs=hbm,
        scratch_shapes=[VMEM((256, 256), bf16)] * 2 + work(1),
        compiler_params=params,
        cost_estimate=pl.CostEstimate(
            flops=2 * 2 * 10 * 128 * 128 * cols, bytes_accessed=4 * rows * cols, transcendentals=0
        ),
        name="own",
    )(own, factor, grad_near, moment_near, *in_hbm(back_wide, pair_tall))

    new_weights = pl.pallas_call(
        finish_kernel,
        out_shape=full,
        in_specs=[whole] + [hbm] * 3,
        out_specs=hbm,
        scratch_shapes=[VMEM((256, 256), bf16)] * 2 + [VMEM((rows, cols), bf16)] + work(replicas),
        compiler_params=params,
        name="finish",
    )(every, *in_hbm(back_wide, pair_tall, weights))
    return (new_momentum[None], new_weights)


def solution(mesh):
    in_specs = (
        P("rep", "fsdp", None),
        P("rep", "fsdp", None),
        P("rep", "fsdp", None),
        P("fsdp", None),
    )
    out_specs = (P("rep", "fsdp", None), P("fsdp", None))
    return jax.shard_map(body, mesh=mesh, in_specs=in_specs, out_specs=out_specs, check_vma=False)
```
